128 devices in a mesh: seq: 16 (over z_lo, y, core), exp: 8 (over z_hi, x).
Axes of the slice: x: 4, y: 4, z: 4 (z_hi: 2, z_lo: 2; z = z_hi * 2 + z_lo), core: 2. Of those that a mesh axis runs over, the one named last changes fastest.
Arguments:
- resid: bfloat16 [16384, 2560], P(('seq', 'exp')), may hold values from -30 to 30
- queries: bfloat16 [16384, 1536], P('seq', 'exp'), may hold values from -6 to 6
- keyvals: bfloat16 [16384, 1024], P('seq', 'exp'), may hold values from -6 to 6
- out_proj: bfloat16 [1536, 2560], replicated, may hold values from -0.15625 to 0.15625
- norm_gain: bfloat16 [2560], replicated, may hold values from 0.099609375 to 1.8984375
- token_ids: int32 [16384], P(('seq', 'exp')), may hold values from 0 to 128255
- hash_table: int32 [128256], replicated, may hold values from 0 to 7
- w_gate: bfloat16 [8, 1024, 2560], P('exp', 'seq'), may hold values from -0.125 to 0.125
- w_up: bfloat16 [8, 1024, 2560], P('exp', 'seq'), may hold values from -0.125 to 0.125
- w_down: bfloat16 [8, 1024, 2560], P('exp', 'seq'), may hold values from -0.1875 to 0.1875
- cotangent: bfloat16 [16384, 2560], P(('seq', 'exp')), may hold values from -0.5 to 0.5
Outputs:
- layer_out: bfloat16 [16384, 2560], P(('seq', 'exp'))
- grad_gate: bfloat16 [8, 1024, 2560], P('exp', 'seq')
- grad_up: bfloat16 [8, 1024, 2560], P('exp', 'seq')
- grad_down: bfloat16 [8, 1024, 2560], P('exp', 'seq')
The draws below stay inside these ranges and needn't reach their ends.
All inputs are finite; a program needn't handle non-finite values.
Results may differ from the reference program's by a relative error of at most 0.03.
Values may be sent and summed in bfloat16 or wider, within the bound.
A program may use at most 128 MiB of HBM per device.

```python
import math
import jax
import jax.numpy as jnp
import numpy as np
from jax import lax

MODEL_DIM = 2560
FF = 1024
QUERY_COUNT = 24
KEYVALUE_HEADS = 8
HEAD_DIM = 64
VOCAB = 128256
SEQ_DEV = 1024
SEQUENCE_LENGTH = 16384
ROUTE_TOKENS = 128
EXPERTS = 8
CAP = 16
N_SEQ = 16


def draw_queries(key, part):
    key = jax.random.fold_in(key, 1)
    value_matrix = jnp.clip(jax.random.normal(key, (SEQUENCE_LENGTH, QUERY_COUNT, HEAD_DIM), jnp.float32), -4.0, 4.0)
    return value_matrix.reshape(SEQUENCE_LENGTH, QUERY_COUNT * HEAD_DIM).astype(jnp.bfloat16)


def draw_keyvals(key, part):
    key = jax.random.fold_in(key, 2)
    value_matrix = jnp.clip(jax.random.normal(key, (SEQUENCE_LENGTH, KEYVALUE_HEADS, 2, HEAD_DIM), jnp.float32), -4.0, 4.0)
    return value_matrix.reshape(SEQUENCE_LENGTH, KEYVALUE_HEADS * 2 * HEAD_DIM).astype(jnp.bfloat16)


def draw_resid(key, part):
    key = jax.random.fold_in(key, 3)
    value_matrix = jnp.clip(jax.random.normal(key, (SEQUENCE_LENGTH, MODEL_DIM), jnp.float32), -5.0, 5.0)
    return value_matrix.astype(jnp.bfloat16)


def touch_ends(result, key, low, high):
    shape = result.shape
    spot = [jax.random.randint(jax.random.fold_in(key, axis), (), 0, shape[axis]) for axis in range(len(shape))]
    result = result.at[tuple(spot)].set(low)
    longest = shape.index(max(shape))
    spot[longest] = (spot[longest] + 1) % shape[longest]
    return result.at[tuple(spot)].set(high)


def steps_of(stream_key, dims, cuts, smallest, high):
    gain, own = 1.0, jax.random.fold_in(stream_key, 6)
    for dim, blocks in cuts:
        draws = jnp.exp(jax.random.uniform(jax.random.fold_in(own, dim), (blocks,), jnp.float32, smallest / len(cuts), high / len(cuts)))
        gain = gain * jnp.repeat(draws, dims[dim] // blocks).reshape([-1 if axis == dim else 1 for axis in range(len(dims))])
    return gain


def ranked_wide(key, extent, count, skew):
    weights = [min(1 << octave, count + 1 - (1 << octave)) * (1 << 20) // math.isqrt((1 << octave) ** skew) + 1 for octave in range((count + 1).bit_length()) if 1 << octave <= count]
    scale = 1 + sum(weights) // (1 << 30)
    table = np.cumsum(np.array([max(1, weight // scale) for weight in weights]))
    ticket = jax.random.randint(jax.random.fold_in(key, 1), extent, 0, int(table[len(weights) - 1]))
    start = jnp.left_shift(1, jnp.searchsorted(jnp.asarray(table, jnp.int32), ticket, side="right").astype(jnp.int32))
    standing = start - 1 + jax.random.randint(jax.random.fold_in(key, 4), extent, 0, 1 << 30) % jnp.minimum(start, count + 1 - start)
    return jax.random.permutation(jax.random.fold_in(key, 2), count)[standing].astype(jnp.int32)


def bell_draw(rng, shape, deviation, limit, pieces=(), kind=jnp.bfloat16):
    loudness = steps_of(rng, shape, pieces, -0.22, 0.18) if pieces else 1.0
    values = jax.random.normal(rng, shape, jnp.float32) * deviation * loudness
    return jnp.minimum(jnp.maximum(values, -limit), limit).astype(kind)


def setup_inputs(seed: int = 0) -> dict:
    key_list = jax.random.split(jax.random.key(seed), 12)
    resid = draw_resid(jax.random.fold_in(key_list[11], 71), 0)
    queries = draw_queries(jax.random.fold_in(key_list[11], 71), 0)
    keyvals = draw_keyvals(jax.random.fold_in(key_list[11], 71), 0)
    out_proj = bell_draw(key_list[3], (QUERY_COUNT * HEAD_DIM, MODEL_DIM), (QUERY_COUNT * HEAD_DIM) ** -0.5, 0.15625)
    norm_gain = jnp.clip(1.0 + 0.18 * jax.random.normal(key_list[4], (MODEL_DIM,), jnp.float32), 0.099609375, 1.8984375).astype(jnp.bfloat16)
    token_ids = touch_ends(ranked_wide(key_list[5], (SEQUENCE_LENGTH,), VOCAB, 2), jax.random.fold_in(key_list[5], 3), 0, VOCAB - 1).astype(jnp.int32)
    hash_table = touch_ends(jax.random.randint(key_list[6], (VOCAB,), 0, EXPERTS), jax.random.fold_in(key_list[6], 1), 0, EXPERTS - 1).astype(jnp.int32)
    w_gate = bell_draw(key_list[7], (EXPERTS, FF, MODEL_DIM), MODEL_DIM ** -0.5, 0.125, ((0, 8), (1, 16)))
    w_up = bell_draw(key_list[8], (EXPERTS, FF, MODEL_DIM), MODEL_DIM ** -0.5, 0.125, ((0, 8), (1, 16)))
    w_down = bell_draw(key_list[9], (EXPERTS, FF, MODEL_DIM), FF ** -0.5, 0.1875, ((0, 8), (1, 16)))
    cotangent = bell_draw(key_list[10], (SEQUENCE_LENGTH, MODEL_DIM), (1.0 / 32), 0.5, ((0, 128),))
    return {"resid": resid, "queries": queries, "keyvals": keyvals, "out_proj": out_proj, "norm_gain": norm_gain, "token_ids": token_ids, "hash_table": hash_table, "w_gate": w_gate, "w_up": w_up, "w_down": w_down, "cotangent": cotangent}


very_negative = -1e+30
norm_eps = 1e-05

def round_trip(value_matrix):
    return lax.optimization_barrier(value_matrix.astype(jnp.bfloat16)).astype(jnp.float32)

def head_attention(query_head, key_head, value_head):
    positions = jnp.arange(SEQUENCE_LENGTH, dtype=jnp.int32)
    score_scale = 1.0 / math.sqrt(HEAD_DIM)
    key_wide = key_head.astype(jnp.float32)
    value_wide = value_head.astype(jnp.float32)

    def query_block(first_row):
        query_rows = lax.dynamic_slice_in_dim(query_head, first_row, SEQ_DEV, 0).astype(jnp.float32)
        scores = jnp.dot(query_rows, key_wide.T) * score_scale
        query_place = first_row + jnp.arange(SEQ_DEV, dtype=jnp.int32)
        allowed = positions[None, :] <= query_place[:, None]
        masked = jnp.where(allowed, scores, very_negative)
        row_max = lax.optimization_barrier(jnp.max(masked, axis=1, keepdims=True))
        weights = jnp.where(allowed, jnp.exp(masked - row_max), 0.0)
        weight_sum = lax.optimization_barrier(jnp.sum(weights, axis=1, keepdims=True))
        mixed_rows = jnp.dot(round_trip(weights), value_wide)
        return mixed_rows / weight_sum
    starts = jnp.arange(N_SEQ, dtype=jnp.int32) * SEQ_DEV
    return lax.map(query_block, starts).reshape(SEQUENCE_LENGTH, HEAD_DIM)

def reference(resid, queries, keyvals, out_proj, norm_gain, token_ids, hash_table, w_gate, w_up, w_down, cotangent):
    query_group_width = QUERY_COUNT // KEYVALUE_HEADS
    query_heads = queries.reshape(SEQUENCE_LENGTH, QUERY_COUNT, HEAD_DIM).transpose(1, 0, 2)
    paired_heads = keyvals.reshape(SEQUENCE_LENGTH, KEYVALUE_HEADS, 2, HEAD_DIM).transpose(1, 2, 0, 3)

    def one_head(head_index):
        pair_block = paired_heads[head_index // query_group_width]
        return head_attention(query_heads[head_index], pair_block[0], pair_block[1])
    head_mixes = lax.map(one_head, jnp.arange(QUERY_COUNT, dtype=jnp.int32))
    attention = head_mixes.transpose(1, 0, 2).reshape(SEQUENCE_LENGTH, QUERY_COUNT * HEAD_DIM).astype(jnp.bfloat16)
    projected = jnp.dot(attention, out_proj, preferred_element_type=jnp.float32)
    hidden_state = (resid.astype(jnp.float32) + projected).astype(jnp.bfloat16)
    widened = hidden_state.astype(jnp.float32)
    mean_square = lax.optimization_barrier(jnp.mean(widened * widened, axis=1, keepdims=True))
    normed = (widened * lax.rsqrt(mean_square + norm_eps) * norm_gain.astype(jnp.float32)).astype(jnp.bfloat16)
    count_of_blocks = SEQUENCE_LENGTH // ROUTE_TOKENS
    expert_of = jnp.take(hash_table, token_ids).astype(jnp.int32).reshape(count_of_blocks, ROUTE_TOKENS)
    onehot_slots = (expert_of[:, :, None] == jnp.arange(EXPERTS, dtype=jnp.int32)[None, None, :]).astype(jnp.int32)
    earlier = jnp.cumsum(onehot_slots, axis=1) - onehot_slots
    slot_of = lax.optimization_barrier(jnp.sum(onehot_slots * earlier, axis=2))
    target = jnp.where(slot_of < CAP, expert_of * CAP + slot_of, -1)
    dispatch_table = (jnp.arange(EXPERTS * CAP, dtype=jnp.int32)[None, :, None] == target[:, None, :]).astype(jnp.float32)

    def arrange(token_matrix):
        placed_rows = jnp.einsum('wvm,wmq->wvq', dispatch_table, token_matrix.reshape(count_of_blocks, ROUTE_TOKENS, MODEL_DIM).astype(jnp.float32))
        placed_rows = placed_rows.reshape(N_SEQ, EXPERTS, EXPERTS, CAP, MODEL_DIM).transpose(0, 2, 1, 3, 4)
        return placed_rows.reshape(N_SEQ, EXPERTS, EXPERTS * CAP, MODEL_DIM).astype(jnp.bfloat16)
    expert_rows = arrange(normed)
    grad_rows = arrange(cotangent)
    gate_wide = w_gate.astype(jnp.float32)
    up_wide = w_up.astype(jnp.float32)
    down_wide = w_down.astype(jnp.float32)

    def shard_step(grad_sums, shard_pair):
        rows_wide = shard_pair[0].astype(jnp.float32)
        grads_wide = shard_pair[1].astype(jnp.float32)
        gate_act = jnp.einsum('erd,efd->erf', rows_wide, gate_wide)
        up_act = jnp.einsum('erd,efd->erf', rows_wide, up_wide)
        sigmoid_gate = jax.nn.sigmoid(gate_act)
        silu_gate = gate_act * sigmoid_gate
        hidden_units = (silu_gate * up_act).astype(jnp.bfloat16)
        expert_out = jnp.einsum('erf,efd->erd', hidden_units.astype(jnp.float32), down_wide).astype(jnp.bfloat16)
        hidden_grad = jnp.einsum('erd,efd->erf', grads_wide, down_wide)
        gate_grad = (hidden_grad * up_act * sigmoid_gate * (1.0 + gate_act * (1.0 - sigmoid_gate))).astype(jnp.bfloat16)
        up_grad = (hidden_grad * silu_gate).astype(jnp.bfloat16)
        part_gate = jnp.einsum('erf,erd->efd', gate_grad.astype(jnp.float32), rows_wide)
        part_up = jnp.einsum('erf,erd->efd', up_grad.astype(jnp.float32), rows_wide)
        part_down = jnp.einsum('erf,erd->efd', hidden_units.astype(jnp.float32), grads_wide)
        new_sums = (grad_sums[0] + round_trip(part_gate), grad_sums[1] + round_trip(part_up), grad_sums[2] + round_trip(part_down))
        return (new_sums, expert_out)
    zero_sums = (jnp.zeros((EXPERTS, FF, MODEL_DIM), jnp.float32), jnp.zeros((EXPERTS, FF, MODEL_DIM), jnp.float32), jnp.zeros((EXPERTS, FF, MODEL_DIM), jnp.float32))
    grad_sums, expert_outs = lax.scan(shard_step, zero_sums, (expert_rows, grad_rows))
    returned_rows = expert_outs.reshape(N_SEQ, EXPERTS, EXPERTS, CAP, MODEL_DIM).transpose(0, 2, 1, 3, 4).reshape(count_of_blocks, EXPERTS * CAP, MODEL_DIM)
    combined_output = jnp.einsum('gyq,gyl->gql', dispatch_table, returned_rows.astype(jnp.float32))
    layer_out = (widened.reshape(count_of_blocks, ROUTE_TOKENS, MODEL_DIM) + combined_output).reshape(SEQUENCE_LENGTH, MODEL_DIM).astype(jnp.bfloat16)
    return (layer_out, grad_sums[0].astype(jnp.bfloat16), grad_sums[1].astype(jnp.bfloat16), grad_sums[2].astype(jnp.bfloat16))
```

```python
import functools
import math

import jax
import jax.numpy as jnp
from jax import lax
from jax.experimental import pallas as pl
from jax.experimental.pallas import tpu as pltpu
from jax.sharding import Mesh
from jax.sharding import PartitionSpec as P

HEAD_DIM = 64
SEQ = ("zl", "y", "c")
UNITS = ("zl", "c")
score_to_log2 = math.log2(math.e) / math.sqrt(HEAD_DIM)
very_negative = -1e30
norm_eps = 1e-05


def contract_rows(first_operand, second_operand):
    return lax.dot_general(
        first_operand, second_operand, (((0,), (0,)), ((), ())), preferred_element_type=jnp.float32
    )


def contract_cols(first_operand, second_operand):
    return lax.dot_general(
        first_operand, second_operand, (((1,), (1,)), ((), ())), preferred_element_type=jnp.float32
    )


def swiglu_forward(gate_act, up_act):
    sigmoid_gate = jax.nn.sigmoid(gate_act)
    silu_gate = gate_act * sigmoid_gate
    return (silu_gate * up_act).astype(jnp.bfloat16)


def swiglu_backward(gate_act, up_act, hidden_grad):
    sigmoid_gate = jax.nn.sigmoid(gate_act)
    silu_gate = gate_act * sigmoid_gate
    gate_grad = (
        hidden_grad * up_act * sigmoid_gate * (1.0 + gate_act * (1.0 - sigmoid_gate))
    ).astype(jnp.bfloat16)
    up_grad = (hidden_grad * silu_gate).astype(jnp.bfloat16)
    return (gate_grad, up_grad)


def attention_kernel(place, q_ref, kv_ref, out_ref, m_ref, acc_ref):
    half_rows = out_ref.shape[1]
    heads = out_ref.shape[2] // HEAD_DIM
    shard_rows = 2 * half_rows
    pieces = half_rows // 128
    ones = jnp.ones((16, half_rows), jnp.bfloat16)

    def values_of(block, part):
        turned = [
            kv_ref[block, pl.ds(half_rows + (part * pieces + j) * HEAD_DIM, HEAD_DIM), :]
            for j in range(pieces)
        ]
        return jnp.concatenate([jnp.concatenate(turned, axis=1), ones], axis=0)

    def step(half, block, parts, masked):
        keys = kv_ref[block, pl.ds(0, half_rows), :]
        scores = []
        for part in range(parts):
            s = (
                jnp.dot(keys, q_ref[half, part], preferred_element_type=jnp.float32)
                * score_to_log2
            )
            if masked and part == parts - 1:
                key_place = lax.broadcasted_iota(jnp.int32, s.shape, 0)
                query_place = lax.broadcasted_iota(jnp.int32, s.shape, 1) % half_rows
                s = jnp.where(key_place <= query_place, s, very_negative)
            scores.append(s)
        old = m_ref[...]
        new = old
        for s in scores:
            new = jnp.maximum(new, jnp.max(s, axis=0, keepdims=True))
        m_ref[...] = new
        total = acc_ref[...] * jnp.exp2(old - new)
        for part, s in enumerate(scores):
            weights = jnp.exp2(s - new).astype(jnp.bfloat16)
            total += jnp.dot(values_of(block, part), weights, preferred_element_type=jnp.float32)
        acc_ref[...] = total

    def run(half, full_blocks, last_parts):
        m_ref[...] = jnp.full_like(m_ref, very_negative)
        acc_ref[...] = jnp.zeros_like(acc_ref)

        def body(block, carry):
            step(half, block, 2, False)
            return carry

        lax.fori_loop(0, full_blocks, body, 0)
        step(half, full_blocks, last_parts, True)
        mixed = acc_ref[pl.ds(0, HEAD_DIM), :] / acc_ref[pl.ds(HEAD_DIM, 1), :]
        for head in range(heads):
            out_ref[half, :, pl.ds(head * HEAD_DIM, HEAD_DIM)] = (
                mixed[:, head * half_rows : (head + 1) * half_rows].T.astype(jnp.bfloat16)
            )

    shard = place[0]
    mirror = place[1]
    run(1, mirror, 2)
    run(0, shard, 1)


def attend(queries, keyvals):
    row_count = queries.shape[0]
    half_rows = row_count // 2
    heads = queries.shape[1] // HEAD_DIM
    shard_count = lax.axis_size(SEQ)
    shard = lax.axis_index(SEQ)
    swap = [(s, shard_count - 1 - s) for s in range(shard_count)]
    keys = keyvals[:, :HEAD_DIM]
    keys = jnp.concatenate([keys[:half_rows], keys[half_rows:]], axis=1)
    values = keyvals[:, HEAD_DIM:].reshape(row_count // 128, 128, HEAD_DIM)
    values = jnp.transpose(values, (0, 2, 1)).reshape(half_rows, 2 * HEAD_DIM)
    packed = jnp.concatenate([keys, values], axis=0)
    gathered = lax.all_gather(packed, SEQ, axis=0, tiled=False)
    odd = lax.ppermute(queries[half_rows:], SEQ, swap)

    def turn(rows):
        turned = jnp.transpose(rows.reshape(half_rows, heads, HEAD_DIM), (2, 1, 0)).reshape(
            HEAD_DIM, heads * half_rows
        )
        empty = jnp.zeros_like(turned)
        return jnp.stack(
            [jnp.concatenate([turned, empty], axis=0), jnp.concatenate([empty, turned], axis=0)]
        )

    turned_queries = jnp.stack([turn(queries[:half_rows]), turn(odd)])
    place = jnp.stack([shard, shard_count - 1 - shard]).astype(jnp.int32)
    mixed = pl.pallas_call(
        attention_kernel,
        out_shape=jax.ShapeDtypeStruct((2, half_rows, heads * HEAD_DIM), jnp.bfloat16),
        in_specs=[
            pl.BlockSpec(memory_space=pltpu.SMEM),
            pl.BlockSpec(memory_space=pltpu.VMEM),
            pl.BlockSpec(memory_space=pltpu.VMEM),
        ],
        out_specs=pl.BlockSpec(memory_space=pltpu.VMEM),
        scratch_shapes=[
            pltpu.VMEM((1, heads * half_rows), jnp.float32),
            pltpu.VMEM((HEAD_DIM + 16, heads * half_rows), jnp.float32),
        ],
        compiler_params=pltpu.CompilerParams(vmem_limit_bytes=48 * 2**20),
        cost_estimate=pl.CostEstimate(
            flops=20_000_000_000, bytes_accessed=6_000_000, transcendentals=27_000_000
        ),
        name="attention",
    )(place, turned_queries, gathered)
    back = lax.ppermute(mixed[1], SEQ, swap)
    return jnp.concatenate([mixed[0], back], axis=0)


def local(
    resid,
    queries,
    keyvals,
    out_proj,
    norm_gain,
    token_ids,
    hash_table,
    w_gate,
    w_up,
    w_down,
    cotangent,
):
    token_count = resid.shape[0]
    model_width = resid.shape[1]
    expert_count = lax.axis_size("exp")
    capacity = token_count // expert_count
    expert_of = jnp.take(hash_table, token_ids)
    onehot_slots = (
        expert_of[:, None] == jnp.arange(expert_count, dtype=jnp.int32)[None, :]
    ).astype(jnp.int32)
    earlier = jnp.cumsum(onehot_slots, axis=0) - onehot_slots
    slot_of = jnp.sum(onehot_slots * earlier, axis=1)
    target = jnp.where(slot_of < capacity, expert_of * capacity + slot_of, -1)
    dispatch_table = (
        jnp.arange(expert_count * capacity, dtype=jnp.int32)[:, None] == target[None, :]
    ).astype(jnp.bfloat16)

    def to_experts(rows):
        sent = (
            jnp.dot(dispatch_table, rows, preferred_element_type=jnp.float32)
            .astype(jnp.bfloat16)
            .reshape(expert_count, capacity, model_width)
        )
        routed = lax.all_to_all(sent, "exp", split_axis=0, concat_axis=0, tiled=True)
        return lax.all_gather(
            routed.reshape(expert_count * capacity, model_width), "y", axis=0, tiled=True
        )

    attention = attend(queries, keyvals)
    output_grads = to_experts(cotangent)
    full_gate, full_up, full_down = (
        lax.all_gather(w[0], UNITS, axis=0, tiled=True) for w in (w_gate, w_up, w_down)
    )
    token_heads = lax.all_to_all(attention, "exp", split_axis=0, concat_axis=1, tiled=True)
    projected = jnp.dot(token_heads, out_proj, preferred_element_type=jnp.float32)
    hidden_state = (resid.astype(jnp.float32) + projected).astype(jnp.bfloat16)
    widened = hidden_state.astype(jnp.float32)
    mean_square = jnp.mean(widened * widened, axis=1, keepdims=True)
    normed = (widened * lax.rsqrt(mean_square + norm_eps) * norm_gain.astype(jnp.float32)).astype(
        jnp.bfloat16
    )
    expert_rows = to_experts(normed)
    gate_act = contract_cols(expert_rows, full_gate)
    up_act = contract_cols(expert_rows, full_up)
    hidden_units = swiglu_forward(gate_act, up_act)
    expert_out = jnp.dot(hidden_units, full_down, preferred_element_type=jnp.float32).astype(
        jnp.bfloat16
    )
    summed_out = lax.psum_scatter(expert_out, "y", scatter_dimension=0, tiled=True)
    hidden_grad = contract_cols(output_grads, full_down)
    gate_grad, up_grad = swiglu_backward(gate_act, up_act, hidden_grad)

    def to_owner(partial):
        return lax.psum_scatter(
            partial.astype(jnp.bfloat16), UNITS, scatter_dimension=0, tiled=True
        )[None]

    grad_gate = to_owner(contract_rows(gate_grad, expert_rows))
    grad_up = to_owner(contract_rows(up_grad, expert_rows))
    grad_down = to_owner(contract_rows(hidden_units, output_grads))
    returned_rows = lax.all_to_all(
        summed_out.reshape(expert_count, capacity, model_width),
        "exp",
        split_axis=0,
        concat_axis=0,
        tiled=True,
    )
    combined_output = contract_rows(
        dispatch_table, returned_rows.reshape(expert_count * capacity, model_width)
    )
    layer_out = (widened + combined_output).astype(jnp.bfloat16)
    return (layer_out, grad_gate, grad_up, grad_down)


def solution(mesh):
    fine_mesh = Mesh(mesh.devices.reshape(2, 4, 2, 8), ("zl", "y", "c", "exp"))
    token_spec = P((*SEQ, "exp"), None)
    weight_spec = P("exp", SEQ, None)
    in_specs = (
        token_spec,
        P(SEQ, "exp"),
        P(SEQ, "exp"),
        P(),
        P(),
        P((*SEQ, "exp")),
        P(),
        weight_spec,
        weight_spec,
        weight_spec,
        token_spec,
    )
    out_specs = (token_spec, weight_spec, weight_spec, weight_spec)
    return jax.shard_map(
        local, mesh=fine_mesh, in_specs=in_specs, out_specs=out_specs, check_vma=False
    )
```

```python
import functools
import math

import jax
import jax.numpy as jnp
from jax import lax
from jax.experimental import pallas as pl
from jax.experimental.pallas import tpu as pltpu
from jax.sharding import Mesh
from jax.sharding import PartitionSpec as P

HEAD_DIM = 64
SEQ = ("zl", "y", "c")
UNITS = ("c", "y")
MESH = pl.DeviceIdType.MESH
score_to_log2 = math.log2(math.e) / math.sqrt(HEAD_DIM)
very_negative = -1e30
norm_eps = 1e-05


def contract_rows(first_operand, second_operand):
    return lax.dot_general(
        first_operand, second_operand, (((0,), (0,)), ((), ())), preferred_element_type=jnp.float32
    )


def contract_cols(first_operand, second_operand):
    return lax.dot_general(
        first_operand, second_operand, (((1,), (1,)), ((), ())), preferred_element_type=jnp.float32
    )


def swiglu_forward(gate_act, up_act):
    sigmoid_gate = jax.nn.sigmoid(gate_act)
    silu_gate = gate_act * sigmoid_gate
    return (silu_gate * up_act).astype(jnp.bfloat16)


def swiglu_backward(gate_act, up_act, hidden_grad):
    sigmoid_gate = jax.nn.sigmoid(gate_act)
    silu_gate = gate_act * sigmoid_gate
    gate_grad = (
        hidden_grad * up_act * sigmoid_gate * (1.0 + gate_act * (1.0 - sigmoid_gate))
    ).astype(jnp.bfloat16)
    up_grad = (hidden_grad * silu_gate).astype(jnp.bfloat16)
    return (gate_grad, up_grad)


def attention_kernel(place, q_ref, kv_ref, out_ref, m_ref, acc_ref):
    half_rows = out_ref.shape[1]
    heads = out_ref.shape[2] // HEAD_DIM
    shard_rows = 2 * half_rows
    pieces = half_rows // 128
    ones = jnp.ones((16, half_rows), jnp.bfloat16)

    def values_of(block, part):
        turned = [
            kv_ref[block, pl.ds(half_rows + (part * pieces + j) * HEAD_DIM, HEAD_DIM), :]
            for j in range(pieces)
        ]
        return jnp.concatenate([jnp.concatenate(turned, axis=1), ones], axis=0)

    def step(half, block, parts, masked):
        keys = kv_ref[block, pl.ds(0, half_rows), :]
        scores = []
        for part in range(parts):
            s = (
                jnp.dot(keys, q_ref[half, part], preferred_element_type=jnp.float32)
                * score_to_log2
            )
            if masked and part == parts - 1:
                key_place = lax.broadcasted_iota(jnp.int32, s.shape, 0)
                query_place = lax.broadcasted_iota(jnp.int32, s.shape, 1) % half_rows
                s = jnp.where(key_place <= query_place, s, very_negative)
            scores.append(s)
        old = m_ref[...]
        new = old
        for s in scores:
            new = jnp.maximum(new, jnp.max(s, axis=0, keepdims=True))
        m_ref[...] = new
        total = acc_ref[...] * jnp.exp2(old - new)
        for part, s in enumerate(scores):
            weights = jnp.exp2(s - new).astype(jnp.bfloat16)
            total += jnp.dot(values_of(block, part), weights, preferred_element_type=jnp.float32)
        acc_ref[...] = total

    def run(half, full_blocks, last_parts):
        m_ref[...] = jnp.full_like(m_ref, very_negative)
        acc_ref[...] = jnp.zeros_like(acc_ref)

        def body(block, carry):
            step(half, block, 2, False)
            return carry

        lax.fori_loop(0, full_blocks, body, 0)
        step(half, full_blocks, last_parts, True)
        mixed = acc_ref[pl.ds(0, HEAD_DIM), :] / acc_ref[pl.ds(HEAD_DIM, 1), :]
        for head in range(heads):
            out_ref[half, :, pl.ds(head * HEAD_DIM, HEAD_DIM)] = (
                mixed[:, head * half_rows : (head + 1) * half_rows].T.astype(jnp.bfloat16)
            )

    shard = place[0]
    mirror = place[1]
    run(1, mirror, 2)
    run(0, shard, 1)


def attend(queries, keyvals):
    row_count = queries.shape[0]
    half_rows = row_count // 2
    heads = queries.shape[1] // HEAD_DIM
    shard_count = lax.axis_size(SEQ)
    shard = lax.axis_index(SEQ)
    swap = [(s, shard_count - 1 - s) for s in range(shard_count)]
    keys = keyvals[:, :HEAD_DIM]
    keys = jnp.concatenate([keys[:half_rows], keys[half_rows:]], axis=1)
    values = keyvals[:, HEAD_DIM:].reshape(row_count // 128, 128, HEAD_DIM)
    values = jnp.transpose(values, (0, 2, 1)).reshape(half_rows, 2 * HEAD_DIM)
    packed = jnp.concatenate([keys, values], axis=0)
    gathered = lax.all_gather(packed, SEQ, axis=0, tiled=False)
    odd = lax.ppermute(queries[half_rows:], SEQ, swap)

    def turn(rows):
        turned = jnp.transpose(rows.reshape(half_rows, heads, HEAD_DIM), (2, 1, 0)).reshape(
            HEAD_DIM, heads * half_rows
        )
        empty = jnp.zeros_like(turned)
        return jnp.stack(
            [jnp.concatenate([turned, empty], axis=0), jnp.concatenate([empty, turned], axis=0)]
        )

    turned_queries = jnp.stack([turn(queries[:half_rows]), turn(odd)])
    place = jnp.stack([shard, shard_count - 1 - shard]).astype(jnp.int32)
    mixed = pl.pallas_call(
        attention_kernel,
        out_shape=jax.ShapeDtypeStruct((2, half_rows, heads * HEAD_DIM), jnp.bfloat16),
        in_specs=[
            pl.BlockSpec(memory_space=pltpu.SMEM),
            pl.BlockSpec(memory_space=pltpu.VMEM),
            pl.BlockSpec(memory_space=pltpu.VMEM),
        ],
        out_specs=pl.BlockSpec(memory_space=pltpu.VMEM),
        scratch_shapes=[
            pltpu.VMEM((1, heads * half_rows), jnp.float32),
            pltpu.VMEM((HEAD_DIM + 16, heads * half_rows), jnp.float32),
        ],
        compiler_params=pltpu.CompilerParams(vmem_limit_bytes=48 * 2**20),
        cost_estimate=pl.CostEstimate(
            flops=20_000_000_000, bytes_accessed=6_000_000, transcendentals=27_000_000
        ),
        name="attention",
    )(place, turned_queries, gathered)
    back = lax.ppermute(mixed[1], SEQ, swap)
    return jnp.concatenate([mixed[0], back], axis=0)


def neighbour(**place):
    return {axis: place.get(axis, lax.axis_index(axis)) for axis in (*SEQ, "exp")}


def expert_kernel(
    rows_ref,
    cot_ref,
    gate_ref,
    up_ref,
    down_ref,
    hidden_ref,
    combine_ref,
    layer_ref,
    grad_gate_ref,
    grad_up_ref,
    grad_down_ref,
    rows_in,
    cot_in,
    out_buf,
    out_in,
    parts,
    core_in,
    sums,
    half_up_in,
    half_down_in,
    full_up_in,
    full_down_in,
    push_send,
    push_recv,
    ring_send,
    ring_recv,
    local_sem,
):
    zl, y, c, ex = (lax.axis_index(a) for a in (*SEQ, "exp"))
    experts = rows_ref.shape[0]
    capacity, width = rows_ref.shape[1:]
    tokens = 2 * experts * capacity
    core_peer = neighbour(c=1 - c)
    y_up = neighbour(y=lax.rem(y + 1, 4))
    y_down = neighbour(y=lax.rem(y + 3, 4))
    offsets = [(dz, de) for dz in range(2) for de in range(experts)]

    def peer(dz, de):
        return lax.rem(zl + dz, 2), lax.rem(ex + de, experts)

    def source(dz, de):
        return lax.rem(zl + 2 - dz, 2), lax.rem(ex + experts - de, experts)

    barrier = pltpu.get_barrier_semaphore()
    for dz, de in offsets[1:]:
        tz, te = peer(dz, de)
        pl.semaphore_signal(
            barrier, inc=1, device_id=neighbour(zl=tz, exp=te), device_id_type=MESH
        )
    for other in (core_peer, y_up, y_down):
        pl.semaphore_signal(barrier, inc=1, device_id=other, device_id_type=MESH)
    pl.semaphore_wait(barrier, len(offsets) + 2)

    def push(kind, index, src, dst, to):
        return pltpu.make_async_remote_copy(
            src_ref=src,
            dst_ref=dst,
            send_sem=push_send.at[kind, index],
            recv_sem=push_recv.at[kind, index],
            device_id=to,
            device_id_type=MESH,
        )

    def spread(kind, src_ref, dst_ref):
        own = pltpu.make_async_copy(src_ref.at[ex], dst_ref.at[zl, ex], local_sem.at[kind])
        own.start()
        sent = []
        for index, (dz, de) in enumerate(offsets):
            if index:
                tz, te = peer(dz, de)
                copy = push(
                    kind, index, src_ref.at[te], dst_ref.at[zl, ex], neighbour(zl=tz, exp=te)
                )
                copy.start()
                sent.append(copy)
        return own, sent

    def arrive(spread_copies):
        own, sent = spread_copies
        own.wait()
        for copy in sent:
            copy.wait_recv()

    cot_copies = spread(0, cot_ref, cot_in)
    rows_copies = spread(1, rows_ref, rows_in)

    def flat(ref):
        return ref[...].reshape(tokens, width)

    def ring(mat, stage, src, dst, to):
        return pltpu.make_async_remote_copy(
            src_ref=src,
            dst_ref=dst,
            send_sem=ring_send.at[mat, stage],
            recv_sem=ring_recv.at[mat, stage],
            device_id=to,
            device_id_type=MESH,
        )

    chunk = 512

    def partial(mat, first, second):
        turned = first.T
        for start in range(0, width, chunk):
            part = jnp.dot(
                turned, second[:, start : start + chunk], preferred_element_type=jnp.float32
            ).astype(jnp.bfloat16)
            parts[mat, :, :, :, pl.ds(start, chunk)] = part.reshape(2, 4, -1, chunk)

    started = []

    def go(copy):
        copy.start()
        started.append(copy)
        return copy

    def core_stage(mat):
        return go(ring(mat, 0, parts.at[mat, 1 - c], core_in.at[mat], core_peer))

    def wide(value):
        return value.astype(jnp.float32)

    half = parts.shape[3] // 2

    def half_stage(mat, core_copy):
        core_copy.wait_recv()
        sums[mat] = (wide(parts[mat, c]) + wide(core_in[mat])).astype(jnp.bfloat16)
        far = lax.rem(y + 2, 4)
        return (
            go(ring(mat, 1, sums.at[mat, far, pl.ds(0, half)], half_up_in.at[mat], y_up)),
            go(ring(mat, 2, sums.at[mat, far, pl.ds(half, half)], half_down_in.at[mat], y_down)),
        )

    def full_stage(mat, copies):
        above = lax.rem(y + 1, 4)
        below = lax.rem(y + 3, 4)
        copies[0].wait_recv()
        low = pl.ds(0, half)
        sums[mat, above, low] = (wide(sums[mat, above, low]) + wide(half_up_in[mat])).astype(
            jnp.bfloat16
        )
        first = go(ring(mat, 3, sums.at[mat, above], full_up_in.at[mat], y_up))
        copies[1].wait_recv()
        high = pl.ds(half, half)
        sums[mat, below, high] = (wide(sums[mat, below, high]) + wide(half_down_in[mat])).astype(
            jnp.bfloat16
        )
        return (first, go(ring(mat, 4, sums.at[mat, below], full_down_in.at[mat], y_down)))

    def finish(mat, copies, out_ref):
        for copy in copies:
            copy.wait_recv()
        out_ref[0] = (wide(sums[mat, y]) + wide(full_up_in[mat]) + wide(full_down_in[mat])).astype(
            jnp.bfloat16
        )

    arrive(cot_copies)
    output_grads = flat(cot_in)
    hidden_grad = contract_cols(output_grads, down_ref[...])
    arrive(rows_copies)
    expert_rows = flat(rows_in)
    gate_act = contract_cols(expert_rows, gate_ref[...])
    up_act = contract_cols(expert_rows, up_ref[...])
    hidden_units = swiglu_forward(gate_act, up_act)
    partial(0, hidden_units, output_grads)
    core_down = core_stage(0)
    gate_grad, up_grad = swiglu_backward(gate_act, up_act, hidden_grad)
    partial(1, gate_grad, expert_rows)
    core_gate = core_stage(1)
    half_down = half_stage(0, core_down)
    partial(2, up_grad, expert_rows)
    core_up = core_stage(2)
    half_gate = half_stage(1, core_gate)
    for start in range(0, width, chunk):
        out_buf[:, :, :, pl.ds(start, chunk)] = (
            jnp.dot(
                hidden_units,
                down_ref[:, pl.ds(start, chunk)],
                preferred_element_type=jnp.float32,
            )
            .astype(jnp.bfloat16)
            .reshape(2, experts, capacity, chunk)
        )
    own_out = pltpu.make_async_copy(out_buf.at[zl, ex], out_in.at[zl, ex], local_sem.at[2])
    own_out.start()
    back = []
    for index, (dz, de) in enumerate(offsets):
        if index:
            tz, te = peer(dz, de)
            copy = push(
                2, index, out_buf.at[tz, te], out_in.at[zl, ex], neighbour(zl=tz, exp=te)
            )
            copy.start()
            back.append(copy)
    full_down = full_stage(0, half_down)
    half_up = half_stage(2, core_up)
    full_gate = full_stage(1, half_gate)
    full_up = full_stage(2, half_up)
    finish(0, full_down, grad_down_ref)
    arrive((own_out, back))
    for start in range(0, width, chunk):
        cols = pl.ds(start, chunk)
        returned = out_in[:, :, :, cols].reshape(tokens, chunk)
        layer_ref[:, cols] = (
            wide(hidden_ref[:, cols])
            + jnp.dot(combine_ref[...], returned, preferred_element_type=jnp.float32)
        ).astype(jnp.bfloat16)
    finish(1, full_gate, grad_gate_ref)
    finish(2, full_up, grad_up_ref)
    for copy in (*cot_copies[1], *rows_copies[1], *back, *started):
        copy.wait_send()


def expert_layer(send_rows, send_grads, weights, hidden_state, dispatch_table):
    experts, capacity, width = send_rows.shape
    units = weights[0].shape[0]
    owned = units // 8
    token_count = hidden_state.shape[0]
    combine = jnp.concatenate([dispatch_table, dispatch_table], axis=0).T
    vmem = pl.BlockSpec(memory_space=pltpu.VMEM)
    bf16 = jnp.bfloat16
    landing = pltpu.VMEM((2, experts, capacity, width), bf16)
    grad_shape = jax.ShapeDtypeStruct((1, owned, width), bf16)
    return pl.pallas_call(
        expert_kernel,
        out_shape=(jax.ShapeDtypeStruct((token_count, width), bf16),) + (grad_shape,) * 3,
        in_specs=[vmem] * 7,
        out_specs=(vmem,) * 4,
        scratch_shapes=[
            landing,
            landing,
            landing,
            landing,
            pltpu.VMEM((3, 2, 4, owned, width), bf16),
            pltpu.VMEM((3, 4, owned, width), bf16),
            pltpu.VMEM((3, 4, owned, width), bf16),
            pltpu.VMEM((3, owned // 2, width), bf16),
            pltpu.VMEM((3, owned // 2, width), bf16),
            pltpu.VMEM((3, owned, width), bf16),
            pltpu.VMEM((3, owned, width), bf16),
            pltpu.SemaphoreType.DMA((3, 2 * experts)),
            pltpu.SemaphoreType.DMA((3, 2 * experts)),
            pltpu.SemaphoreType.DMA((3, 5)),
            pltpu.SemaphoreType.DMA((3, 5)),
            pltpu.SemaphoreType.DMA((3,)),
        ],
        compiler_params=pltpu.CompilerParams(
            collective_id=1, has_side_effects=True, vmem_limit_bytes=56 * 2**20
        ),
        cost_estimate=pl.CostEstimate(
            flops=5_000_000_000, bytes_accessed=20_000_000, transcendentals=200_000
        ),
        name="experts",
    )(send_rows, send_grads, *weights, hidden_state, combine)


def local(
    resid,
    queries,
    keyvals,
    out_proj,
    norm_gain,
    token_ids,
    hash_table,
    w_gate,
    w_up,
    w_down,
    cotangent,
):
    token_count = resid.shape[0]
    model_width = resid.shape[1]
    expert_count = lax.axis_size("exp")
    capacity = token_count // expert_count
    expert_of = jnp.take(hash_table, token_ids)
    onehot_slots = (
        expert_of[:, None] == jnp.arange(expert_count, dtype=jnp.int32)[None, :]
    ).astype(jnp.int32)
    earlier = jnp.cumsum(onehot_slots, axis=0) - onehot_slots
    slot_of = jnp.sum(onehot_slots * earlier, axis=1)
    target = jnp.where(slot_of < capacity, expert_of * capacity + slot_of, -1)
    dispatch_table = (
        jnp.arange(expert_count * capacity, dtype=jnp.int32)[:, None] == target[None, :]
    ).astype(jnp.bfloat16)

    def placed(rows):
        return (
            jnp.dot(dispatch_table, rows, preferred_element_type=jnp.float32)
            .astype(jnp.bfloat16)
            .reshape(expert_count, capacity, model_width)
        )

    attention = attend(queries, keyvals)
    weights = [lax.all_gather(w[0], UNITS, axis=0, tiled=True) for w in (w_gate, w_up, w_down)]
    token_heads = lax.all_to_all(attention, "exp", split_axis=0, concat_axis=1, tiled=True)
    projected = jnp.dot(token_heads, out_proj, preferred_element_type=jnp.float32)
    hidden_state = (resid.astype(jnp.float32) + projected).astype(jnp.bfloat16)
    widened = hidden_state.astype(jnp.float32)
    mean_square = jnp.mean(widened * widened, axis=1, keepdims=True)
    normed = (widened * lax.rsqrt(mean_square + norm_eps) * norm_gain.astype(jnp.float32)).astype(
        jnp.bfloat16
    )
    return expert_layer(placed(normed), placed(cotangent), weights, hidden_state, dispatch_table)


def solution(mesh):
    fine_mesh = Mesh(mesh.devices.reshape(2, 4, 2, 8), ("zl", "y", "c", "exp"))
    token_spec = P((*SEQ, "exp"), None)
    weight_spec = P("exp", SEQ, None)
    in_specs = (
        token_spec,
        P(SEQ, "exp"),
        P(SEQ, "exp"),
        P(),
        P(),
        P((*SEQ, "exp")),
        P(),
        weight_spec,
        weight_spec,
        weight_spec,
        token_spec,
    )
    out_specs = (token_spec, weight_spec, weight_spec, weight_spec)
    return jax.shard_map(
        local, mesh=fine_mesh, in_specs=in_specs, out_specs=out_specs, check_vma=False
    )
```

```python
import functools
import math

import jax
import jax.numpy as jnp
from jax import lax
from jax.experimental import pallas as pl
from jax.experimental.pallas import tpu as pltpu
from jax.sharding import Mesh
from jax.sharding import PartitionSpec as P

HEAD_DIM = 64
SEQ = ("zl", "y", "c")
MESH = pl.DeviceIdType.MESH
score_to_log2 = math.log2(math.e) / math.sqrt(HEAD_DIM)
very_negative = -1e30
norm_eps = 1e-05


def contract_rows(first_operand, second_operand):
    return lax.dot_general(
        first_operand, second_operand, (((0,), (0,)), ((), ())), preferred_element_type=jnp.float32
    )


def contract_cols(first_operand, second_operand):
    return lax.dot_general(
        first_operand, second_operand, (((1,), (1,)), ((), ())), preferred_element_type=jnp.float32
    )


def swiglu_forward(gate_act, up_act):
    sigmoid_gate = jax.nn.sigmoid(gate_act)
    silu_gate = gate_act * sigmoid_gate
    return (silu_gate * up_act).astype(jnp.bfloat16)


def swiglu_backward(gate_act, up_act, hidden_grad):
    sigmoid_gate = jax.nn.sigmoid(gate_act)
    silu_gate = gate_act * sigmoid_gate
    gate_grad = (
        hidden_grad * up_act * sigmoid_gate * (1.0 + gate_act * (1.0 - sigmoid_gate))
    ).astype(jnp.bfloat16)
    up_grad = (hidden_grad * silu_gate).astype(jnp.bfloat16)
    return (gate_grad, up_grad)


def neighbour(**place):
    return {axis: place.get(axis, lax.axis_index(axis)) for axis in (*SEQ, "exp")}


ARRIVALS = (
    (0, 0, 0),
    (0, 0, 1),
    (1, 0, 0),
    (0, 3, 0),
    (0, 1, 0),
    (1, 1, 0),
    (1, 3, 0),
    (0, 2, 0),
    (1, 2, 0),
    (1, 0, 1),
    (0, 3, 1),
    (0, 1, 1),
    (1, 1, 1),
    (1, 3, 1),
    (0, 2, 1),
    (1, 2, 1),
)
WEIGHTS_START = 1
WEIGHTS_PASS = 13


def attention_kernel(
    queries_ref,
    keyvals_ref,
    grads_ref,
    gate_ref,
    up_ref,
    down_ref,
    heads_out,
    grads_out,
    weights_out,
    kv_all,
    odd_in,
    turned,
    m_ref,
    acc_ref,
    mixed_ref,
    kv_send,
    kv_recv,
    odd_sem,
    push_send,
    push_recv,
    heads_send,
    heads_recv,
    weight_send,
    weight_recv,
    local_sem,
):
    zl, y, c, ex = (lax.axis_index(a) for a in (*SEQ, "exp"))
    half_rows = odd_in.shape[0]
    heads = odd_in.shape[1] // HEAD_DIM
    pieces = half_rows // 128
    experts = grads_ref.shape[0]
    shard = zl * 8 + y * 2 + c
    mirror = 15 - shard
    core_peer = neighbour(c=1 - c)
    z_peer = neighbour(zl=1 - zl)
    y_up = neighbour(y=lax.rem(y + 1, 4))
    y_down = neighbour(y=lax.rem(y + 3, 4))

    def mirrored(e):
        return {"zl": 1 - zl, "y": 3 - y, "c": 1 - c, "exp": e}

    barrier = pltpu.get_barrier_semaphore()
    greeted = [core_peer, y_up, y_down]
    for d in range(experts):
        e = lax.rem(ex + d, experts)
        greeted += [mirrored(e), neighbour(zl=1 - zl, exp=e)]
        if d:
            greeted.append(neighbour(exp=e))
    for other in greeted:
        pl.semaphore_signal(barrier, inc=1, device_id=other, device_id_type=MESH)

    own_weights = [
        pltpu.make_async_copy(ref.at[0], weights_out.at[n, c, y], local_sem.at[n])
        for n, ref in enumerate((gate_ref, up_ref, down_ref))
    ]
    own_grads = pltpu.make_async_copy(grads_ref.at[ex], grads_out.at[zl, ex], local_sem.at[3])
    for copy in (*own_weights, own_grads):
        copy.start()

    keyvals = keyvals_ref[...]
    kv_all[shard, pl.ds(0, half_rows), :] = jnp.concatenate(
        [keyvals[:half_rows, :HEAD_DIM], keyvals[half_rows:, :HEAD_DIM]], axis=1
    )
    values = keyvals.T[HEAD_DIM:]
    for p in range(2 * pieces):
        kv_all[shard, pl.ds(half_rows + p * HEAD_DIM, HEAD_DIM), :] = values[
            :, p * 128 : (p + 1) * 128
        ]

    def turn(half, rows):
        flipped = rows.T
        flat = jnp.concatenate(
            [flipped[h * HEAD_DIM : (h + 1) * HEAD_DIM] for h in range(heads)], axis=1
        )
        empty = jnp.zeros_like(flat)
        turned[half, 0] = jnp.concatenate([flat, empty], axis=0)
        turned[half, 1] = jnp.concatenate([empty, flat], axis=0)

    turn(0, queries_ref[pl.ds(0, half_rows), :])
    m_ref[...] = jnp.full_like(m_ref, very_negative)
    acc_ref[...] = jnp.zeros_like(acc_ref)
    pl.semaphore_wait(barrier, len(greeted))

    odd_copy = pltpu.make_async_remote_copy(
        src_ref=queries_ref.at[pl.ds(half_rows, half_rows)],
        dst_ref=odd_in,
        send_sem=odd_sem.at[0],
        recv_sem=odd_sem.at[1],
        device_id=mirrored(ex),
        device_id_type=MESH,
    )

    def shard_at(dz, dy, dc):
        return lax.rem(zl + dz, 2) * 8 + lax.rem(y + dy, 4) * 2 + lax.rem(c + dc, 2)

    def pass_on(index, t, to):
        return pltpu.make_async_remote_copy(
            src_ref=kv_all.at[t],
            dst_ref=kv_all.at[t],
            send_sem=kv_send.at[index],
            recv_sem=kv_recv.at[t],
            device_id=to,
            device_id_type=MESH,
        )

    routes = {
        (0, 0, 0): (z_peer, y_up, y_down, core_peer),
        (1, 0, 0): (y_up, y_down, core_peer),
        (0, 3, 0): (y_up, core_peer),
        (0, 1, 0): (core_peer,),
        (1, 1, 0): (y_down, core_peer),
        (1, 3, 0): (core_peer,),
        (0, 2, 0): (core_peer,),
        (1, 2, 0): (core_peer,),
    }
    forwards = {}
    for place, targets in routes.items():
        first = sum(len(f) for f in forwards.values())
        forwards[place] = [
            pass_on(first + n, shard_at(*place), to) for n, to in enumerate(targets)
        ]

    def weight_copy(index, rows, dy, to, dc=0):
        part = weights_out.at[:, lax.rem(c + dc, 2), lax.rem(y + dy, 4), rows]
        return pltpu.make_async_remote_copy(
            src_ref=part,
            dst_ref=part,
            send_sem=weight_send.at[index],
            recv_sem=weight_recv.at[index],
            device_id=to,
            device_id_type=MESH,
        )

    owned = weights_out.shape[3]
    every, low, high = pl.ds(0, owned), pl.ds(0, owned // 2), pl.ds(owned // 2, owned // 2)
    weight_own = [
        weight_copy(0, every, 0, y_up),
        weight_copy(1, every, 0, y_down),
        weight_copy(2, every, 0, core_peer),
    ]
    weight_above = weight_copy(3, low, 3, y_up)
    weight_below = weight_copy(4, high, 1, y_down)
    weight_core = [
        weight_copy(5, every, 3, core_peer),
        weight_copy(6, every, 1, core_peer),
        weight_copy(7, every, 2, core_peer),
    ]

    pushes = []
    for index in range(1, 2 * experts):
        dz, de = divmod(index, experts)
        e = lax.rem(ex + de, experts)
        pushes.append(
            pltpu.make_async_remote_copy(
                src_ref=grads_ref.at[e],
                dst_ref=grads_out.at[zl, ex],
                send_sem=push_send.at[index],
                recv_sem=push_recv.at[index],
                device_id=neighbour(zl=lax.rem(zl + dz, 2), exp=e),
                device_id_type=MESH,
            )
        )

    for copy in forwards[(0, 0, 0)]:
        copy.start()
    odd_copy.start()

    ones = jnp.ones((16, half_rows), jnp.bfloat16)

    def values_of(block, part):
        turned_values = [
            kv_all[block, pl.ds(half_rows + (part * pieces + p) * HEAD_DIM, HEAD_DIM), :]
            for p in range(pieces)
        ]
        return jnp.concatenate([jnp.concatenate(turned_values, axis=1), ones], axis=0)

    def step(half, block, parts, masked):
        keys = kv_all[block, pl.ds(0, half_rows), :]
        scores = []
        for part in range(parts):
            s = (
                jnp.dot(keys, turned[half, part], preferred_element_type=jnp.float32)
                * score_to_log2
            )
            if masked and part == parts - 1:
                key_place = lax.broadcasted_iota(jnp.int32, s.shape, 0)
                query_place = lax.broadcasted_iota(jnp.int32, s.shape, 1) % half_rows
                s = jnp.where(key_place <= query_place, s, very_negative)
            scores.append(s)
        old = m_ref[half]
        new = old
        for s in scores:
            new = jnp.maximum(new, jnp.max(s, axis=0, keepdims=True))
        m_ref[half] = new
        total = acc_ref[half] * jnp.exp2(old - new)
        for part, s in enumerate(scores):
            weights = jnp.exp2(s - new).astype(jnp.bfloat16)
            total += jnp.dot(values_of(block, part), weights, preferred_element_type=jnp.float32)
        acc_ref[half] = total

    step(0, shard, 1, True)
    odd_copy.wait_recv()
    turn(1, odd_in[...])

    def visit(slot, carry):
        def pick(axis):
            return sum(
                jnp.where(slot == n, place[axis], 0) for n, place in enumerate(ARRIVALS)
            )

        t = shard_at(pick(0), pick(1), pick(2))

        @pl.when(slot > 0)
        def _():
            pass_on(0, t, core_peer).wait_recv()

        for n, place in enumerate(ARRIVALS):
            if n and place in forwards:

                @pl.when(slot == n)
                def _():
                    for copy in forwards[place]:
                        copy.start()

        @pl.when(slot == WEIGHTS_START)
        def _():
            for copy in own_weights:
                copy.wait()
            for copy in (*weight_own, *pushes):
                copy.start()

        @pl.when(slot == WEIGHTS_PASS)
        def _():
            weight_own[0].wait_recv()
            weight_above.start()
            weight_core[0].start()
            weight_own[1].wait_recv()
            weight_below.start()
            weight_core[1].start()

        def one_half(half, inner):
            @pl.when(t < jnp.where(half == 0, shard, mirror))
            def _():
                step(half, t, 2, False)

            return inner

        lax.fori_loop(0, 2, one_half, 0)
        return carry

    lax.fori_loop(0, len(ARRIVALS), visit, 0)
    step(1, mirror, 2, True)

    for half in range(2):
        total = acc_ref[half]
        mixed = total[:HEAD_DIM] / total[HEAD_DIM : HEAD_DIM + 1]
        for head in range(heads):
            mixed_ref[half, :, pl.ds(head * HEAD_DIM, HEAD_DIM)] = (
                mixed[:, head * half_rows : (head + 1) * half_rows].T.astype(jnp.bfloat16)
            )

    def head_copy(half, block, to):
        return pltpu.make_async_remote_copy(
            src_ref=mixed_ref.at[half, pl.ds(pl.multiple_of(block * 128, 128), 128)],
            dst_ref=heads_out.at[ex],
            send_sem=heads_send.at[half, block],
            recv_sem=heads_recv.at[ex],
            device_id=to,
            device_id_type=MESH,
        )

    even_copies = []
    for d in range(4):
        block = lax.rem(ex + d, 4)
        even_copies.append(head_copy(0, block, neighbour(exp=block)))
    odd_copies = []
    for d in range(4):
        block = lax.rem(ex + d, 4)
        odd_copies.append(head_copy(1, block, mirrored(4 + block)))
    own_heads = pltpu.make_async_copy(
        mixed_ref.at[0, pl.ds(pl.multiple_of(lax.rem(ex, 4) * 128, 128), 128)],
        heads_out.at[ex],
        local_sem.at[4],
    )
    for copy in (*odd_copies, *even_copies[1:]):
        copy.start()

    @pl.when(ex < 4)
    def _():
        own_heads.start()

    @pl.when(ex >= 4)
    def _():
        even_copies[0].start()

    weight_above.wait_recv()
    weight_below.wait_recv()
    weight_core[2].start()

    def head_arrival(e):
        return pltpu.make_async_remote_copy(
            src_ref=mixed_ref.at[0, pl.ds(0, 128)],
            dst_ref=heads_out.at[e],
            send_sem=heads_send.at[0, 0],
            recv_sem=heads_recv.at[e],
            device_id=core_peer,
            device_id_type=MESH,
        )

    for d in range(1, experts):
        head_arrival(lax.rem(ex + d, experts)).wait_recv()

    @pl.when(ex < 4)
    def _():
        own_heads.wait()

    @pl.when(ex >= 4)
    def _():
        head_arrival(ex).wait_recv()
        even_copies[0].wait_send()

    own_grads.wait()
    for copy in pushes:
        copy.wait()
    weight_own[2].wait_recv()
    for copy in weight_core:
        copy.wait_recv()
    odd_copy.wait_send()
    for copies in forwards.values():
        for copy in copies:
            copy.wait_send()
    for copy in (*weight_own, weight_above, weight_below, *weight_core):
        copy.wait_send()
    for copy in (*odd_copies, *even_copies[1:]):
        copy.wait_send()


def attend(queries, keyvals, send_grads, w_gate, w_up, w_down):
    row_count, query_width = queries.shape
    half_rows = row_count // 2
    heads = query_width // HEAD_DIM
    experts, capacity, width = send_grads.shape
    owned = w_gate.shape[1]
    bf16 = jnp.bfloat16
    vmem = pl.BlockSpec(memory_space=pltpu.VMEM)
    anywhere = pl.BlockSpec(memory_space=pl.ANY)
    dma = pltpu.SemaphoreType.DMA
    return pl.pallas_call(
        attention_kernel,
        out_shape=(
            jax.ShapeDtypeStruct((experts, row_count // experts, query_width), bf16),
            jax.ShapeDtypeStruct((2, experts, capacity, width), bf16),
            jax.ShapeDtypeStruct((3, 2, 4, owned, width), bf16),
        ),
        in_specs=[vmem] * 2 + [anywhere] * 4,
        out_specs=(anywhere,) * 3,
        scratch_shapes=[
            pltpu.VMEM((len(ARRIVALS), row_count, 2 * HEAD_DIM), bf16),
            pltpu.VMEM((half_rows, query_width), bf16),
            pltpu.VMEM((2, 2, 2 * HEAD_DIM, heads * half_rows), bf16),
            pltpu.VMEM((2, 1, heads * half_rows), jnp.float32),
            pltpu.VMEM((2, HEAD_DIM + 16, heads * half_rows), jnp.float32),
            pltpu.VMEM((2, half_rows, query_width), bf16),
            dma((15,)),
            dma((len(ARRIVALS),)),
            dma((2,)),
            dma((2 * experts,)),
            dma((2 * experts,)),
            dma((2, 4)),
            dma((experts,)),
            dma((8,)),
            dma((8,)),
            dma((5,)),
        ],
        compiler_params=pltpu.CompilerParams(
            collective_id=0, has_side_effects=True, vmem_limit_bytes=48 * 2**20
        ),
        cost_estimate=pl.CostEstimate(
            flops=20_000_000_000, bytes_accessed=20_000_000, transcendentals=27_000_000
        ),
        name="attention",
    )(queries, keyvals, send_grads, w_gate, w_up, w_down)


def expert_kernel(
    rows_ref,
    cot_in,
    weights_ref,
    hidden_ref,
    combine_ref,
    layer_ref,
    grad_gate_ref,
    grad_up_ref,
    grad_down_ref,
    rows_in,
    out_buf,
    out_in,
    parts,
    core_in,
    sums,
    half_up_in,
    half_down_in,
    full_up_in,
    full_down_in,
    push_send,
    push_recv,
    ring_send,
    ring_recv,
    local_sem,
):
    zl, y, c, ex = (lax.axis_index(a) for a in (*SEQ, "exp"))
    experts = rows_ref.shape[0]
    capacity, width = rows_ref.shape[1:]
    tokens = 2 * experts * capacity
    core_peer = neighbour(c=1 - c)
    y_up = neighbour(y=lax.rem(y + 1, 4))
    y_down = neighbour(y=lax.rem(y + 3, 4))
    offsets = [(dz, de) for dz in range(2) for de in range(experts)]

    def peer(dz, de):
        return lax.rem(zl + dz, 2), lax.rem(ex + de, experts)

    def source(dz, de):
        return lax.rem(zl + 2 - dz, 2), lax.rem(ex + experts - de, experts)

    barrier = pltpu.get_barrier_semaphore()
    for dz, de in offsets[1:]:
        tz, te = peer(dz, de)
        pl.semaphore_signal(
            barrier, inc=1, device_id=neighbour(zl=tz, exp=te), device_id_type=MESH
        )
    for other in (core_peer, y_up, y_down):
        pl.semaphore_signal(barrier, inc=1, device_id=other, device_id_type=MESH)
    pl.semaphore_wait(barrier, len(offsets) + 2)

    def push(kind, index, src, dst, to):
        return pltpu.make_async_remote_copy(
            src_ref=src,
            dst_ref=dst,
            send_sem=push_send.at[kind, index],
            recv_sem=push_recv.at[kind, index],
            device_id=to,
            device_id_type=MESH,
        )

    def spread(kind, src_ref, dst_ref):
        own = pltpu.make_async_copy(src_ref.at[ex], dst_ref.at[zl, ex], local_sem.at[kind])
        own.start()
        sent = []
        for index, (dz, de) in enumerate(offsets):
            if index:
                tz, te = peer(dz, de)
                copy = push(
                    kind, index, src_ref.at[te], dst_ref.at[zl, ex], neighbour(zl=tz, exp=te)
                )
                copy.start()
                sent.append(copy)
        return own, sent

    def arrive(spread_copies):
        own, sent = spread_copies
        own.wait()
        for copy in sent:
            copy.wait_recv()

    rows_copies = spread(1, rows_ref, rows_in)

    def flat(ref):
        return ref[...].reshape(tokens, width)

    def ring(mat, stage, src, dst, to):
        return pltpu.make_async_remote_copy(
            src_ref=src,
            dst_ref=dst,
            send_sem=ring_send.at[mat, stage],
            recv_sem=ring_recv.at[mat, stage],
            device_id=to,
            device_id_type=MESH,
        )

    chunk = 512

    def partial(mat, first, second):
        turned = first.T
        for start in range(0, width, chunk):
            part = jnp.dot(
                turned, second[:, start : start + chunk], preferred_element_type=jnp.float32
            ).astype(jnp.bfloat16)
            parts[mat, :, :, :, pl.ds(start, chunk)] = part.reshape(2, 4, -1, chunk)

    started = []

    def go(copy):
        copy.start()
        started.append(copy)
        return copy

    def core_stage(mat):
        return go(ring(mat, 0, parts.at[mat, 1 - c], core_in.at[mat], core_peer))

    def wide(value):
        return value.astype(jnp.float32)

    half = parts.shape[3] // 2

    def half_stage(mat, core_copy):
        core_copy.wait_recv()
        sums[mat] = (wide(parts[mat, c]) + wide(core_in[mat])).astype(jnp.bfloat16)
        far = lax.rem(y + 2, 4)
        return (
            go(ring(mat, 1, sums.at[mat, far, pl.ds(0, half)], half_up_in.at[mat], y_up)),
            go(ring(mat, 2, sums.at[mat, far, pl.ds(half, half)], half_down_in.at[mat], y_down)),
        )

    def full_stage(mat, copies):
        above = lax.rem(y + 1, 4)
        below = lax.rem(y + 3, 4)
        copies[0].wait_recv()
        low = pl.ds(0, half)
        sums[mat, above, low] = (wide(sums[mat, above, low]) + wide(half_up_in[mat])).astype(
            jnp.bfloat16
        )
        first = go(ring(mat, 3, sums.at[mat, above], full_up_in.at[mat], y_up))
        copies[1].wait_recv()
        high = pl.ds(half, half)
        sums[mat, below, high] = (wide(sums[mat, below, high]) + wide(half_down_in[mat])).astype(
            jnp.bfloat16
        )
        return (first, go(ring(mat, 4, sums.at[mat, below], full_down_in.at[mat], y_down)))

    def finish(mat, copies, out_ref):
        for copy in copies:
            copy.wait_recv()
        out_ref[0] = (wide(sums[mat, y]) + wide(full_up_in[mat]) + wide(full_down_in[mat])).astype(
            jnp.bfloat16
        )

    gate, up, down = (weights_ref[n].reshape(-1, width) for n in range(3))
    output_grads = flat(cot_in)
    hidden_grad = contract_cols(output_grads, down)
    arrive(rows_copies)
    expert_rows = flat(rows_in)
    gate_act = contract_cols(expert_rows, gate)
    up_act = contract_cols(expert_rows, up)
    hidden_units = swiglu_forward(gate_act, up_act)
    partial(0, hidden_units, output_grads)
    core_down = core_stage(0)
    gate_grad, up_grad = swiglu_backward(gate_act, up_act, hidden_grad)
    partial(1, gate_grad, expert_rows)
    core_gate = core_stage(1)
    half_down = half_stage(0, core_down)
    partial(2, up_grad, expert_rows)
    core_up = core_stage(2)
    half_gate = half_stage(1, core_gate)
    for start in range(0, width, chunk):
        out_buf[:, :, :, pl.ds(start, chunk)] = (
            jnp.dot(
                hidden_units,
                down[:, start : start + chunk],
                preferred_element_type=jnp.float32,
            )
            .astype(jnp.bfloat16)
            .reshape(2, experts, capacity, chunk)
        )
    own_out = pltpu.make_async_copy(out_buf.at[zl, ex], out_in.at[zl, ex], local_sem.at[2])
    own_out.start()
    back = []
    for index, (dz, de) in enumerate(offsets):
        if index:
            tz, te = peer(dz, de)
            copy = push(
                2, index, out_buf.at[tz, te], out_in.at[zl, ex], neighbour(zl=tz, exp=te)
            )
            copy.start()
            back.append(copy)
    full_down = full_stage(0, half_down)
    half_up = half_stage(2, core_up)
    full_gate = full_stage(1, half_gate)
    full_up = full_stage(2, half_up)
    finish(0, full_down, grad_down_ref)
    arrive((own_out, back))
    for start in range(0, width, chunk):
        cols = pl.ds(start, chunk)
        returned = out_in[:, :, :, cols].reshape(tokens, chunk)
        layer_ref[:, cols] = (
            wide(hidden_ref[:, cols])
            + jnp.dot(combine_ref[...], returned, preferred_element_type=jnp.float32)
        ).astype(jnp.bfloat16)
    finish(1, full_gate, grad_gate_ref)
    finish(2, full_up, grad_up_ref)
    for copy in (*rows_copies[1], *back, *started):
        copy.wait_send()


def expert_layer(send_rows, grad_rows, weights, hidden_state, dispatch_table):
    experts, capacity, width = send_rows.shape
    owned = weights.shape[3]
    token_count = hidden_state.shape[0]
    combine = jnp.concatenate([dispatch_table, dispatch_table], axis=0).T
    vmem = pl.BlockSpec(memory_space=pltpu.VMEM)
    bf16 = jnp.bfloat16
    landing = pltpu.VMEM((2, experts, capacity, width), bf16)
    grad_shape = jax.ShapeDtypeStruct((1, owned, width), bf16)
    return pl.pallas_call(
        expert_kernel,
        out_shape=(jax.ShapeDtypeStruct((token_count, width), bf16),) + (grad_shape,) * 3,
        in_specs=[vmem] * 5,
        out_specs=(vmem,) * 4,
        scratch_shapes=[
            landing,
            landing,
            landing,
            pltpu.VMEM((3, 2, 4, owned, width), bf16),
            pltpu.VMEM((3, 4, owned, width), bf16),
            pltpu.VMEM((3, 4, owned, width), bf16),
            pltpu.VMEM((3, owned // 2, width), bf16),
            pltpu.VMEM((3, owned // 2, width), bf16),
            pltpu.VMEM((3, owned, width), bf16),
            pltpu.VMEM((3, owned, width), bf16),
            pltpu.SemaphoreType.DMA((3, 2 * experts)),
            pltpu.SemaphoreType.DMA((3, 2 * experts)),
            pltpu.SemaphoreType.DMA((3, 5)),
            pltpu.SemaphoreType.DMA((3, 5)),
            pltpu.SemaphoreType.DMA((3,)),
        ],
        compiler_params=pltpu.CompilerParams(
            collective_id=1, has_side_effects=True, vmem_limit_bytes=56 * 2**20
        ),
        cost_estimate=pl.CostEstimate(
            flops=5_000_000_000, bytes_accessed=20_000_000, transcendentals=200_000
        ),
        name="experts",
    )(send_rows, grad_rows, weights, hidden_state, combine)


def local(
    resid,
    queries,
    keyvals,
    out_proj,
    norm_gain,
    token_ids,
    hash_table,
    w_gate,
    w_up,
    w_down,
    cotangent,
):
    token_count = resid.shape[0]
    model_width = resid.shape[1]
    expert_count = lax.axis_size("exp")
    capacity = token_count // expert_count
    expert_of = jnp.take(hash_table, token_ids)
    onehot_slots = (
        expert_of[:, None] == jnp.arange(expert_count, dtype=jnp.int32)[None, :]
    ).astype(jnp.int32)
    earlier = jnp.cumsum(onehot_slots, axis=0) - onehot_slots
    slot_of = jnp.sum(onehot_slots * earlier, axis=1)
    target = jnp.where(slot_of < capacity, expert_of * capacity + slot_of, -1)
    dispatch_table = (
        jnp.arange(expert_count * capacity, dtype=jnp.int32)[:, None] == target[None, :]
    ).astype(jnp.bfloat16)

    def placed(rows):
        return (
            jnp.dot(dispatch_table, rows, preferred_element_type=jnp.float32)
            .astype(jnp.bfloat16)
            .reshape(expert_count, capacity, model_width)
        )

    token_heads, grad_rows, weights = attend(
        queries, keyvals, placed(cotangent), w_gate, w_up, w_down
    )
    projected = jnp.dot(
        jnp.transpose(token_heads, (1, 0, 2)).reshape(token_count, -1),
        out_proj,
        preferred_element_type=jnp.float32,
    )
    hidden_state = (resid.astype(jnp.float32) + projected).astype(jnp.bfloat16)
    widened = hidden_state.astype(jnp.float32)
    mean_square = jnp.mean(widened * widened, axis=1, keepdims=True)
    normed = (widened * lax.rsqrt(mean_square + norm_eps) * norm_gain.astype(jnp.float32)).astype(
        jnp.bfloat16
    )
    return expert_layer(placed(normed), grad_rows, weights, hidden_state, dispatch_table)


def solution(mesh):
    fine_mesh = Mesh(mesh.devices.reshape(2, 4, 2, 8), ("zl", "y", "c", "exp"))
    token_spec = P((*SEQ, "exp"), None)
    weight_spec = P("exp", SEQ, None)
    in_specs = (
        token_spec,
        P(SEQ, "exp"),
        P(SEQ, "exp"),
        P(),
        P(),
        P((*SEQ, "exp")),
        P(),
        weight_spec,
        weight_spec,
        weight_spec,
        token_spec,
    )
    out_specs = (token_spec, weight_spec, weight_spec, weight_spec)
    return jax.shard_map(
        local, mesh=fine_mesh, in_specs=in_specs, out_specs=out_specs, check_vma=False
    )
```

```python
import functools
import math

import jax
import jax.numpy as jnp
from jax import lax
from jax.experimental import pallas as pl
from jax.experimental.pallas import tpu as pltpu
from jax.sharding import Mesh
from jax.sharding import PartitionSpec as P

HEAD_DIM = 64
SEQ = ("zl", "y", "c")
MESH = pl.DeviceIdType.MESH
score_to_log2 = math.log2(math.e) / math.sqrt(HEAD_DIM)
very_negative = -1e30
norm_eps = 1e-05


def contract_rows(first_operand, second_operand):
    return lax.dot_general(
        first_operand, second_operand, (((0,), (0,)), ((), ())), preferred_element_type=jnp.float32
    )


def contract_cols(first_operand, second_operand):
    return lax.dot_general(
        first_operand, second_operand, (((1,), (1,)), ((), ())), preferred_element_type=jnp.float32
    )


def swiglu_forward(gate_act, up_act):
    sigmoid_gate = jax.nn.sigmoid(gate_act)
    silu_gate = gate_act * sigmoid_gate
    return (silu_gate * up_act).astype(jnp.bfloat16)


def swiglu_backward(gate_act, up_act, hidden_grad):
    sigmoid_gate = jax.nn.sigmoid(gate_act)
    silu_gate = gate_act * sigmoid_gate
    gate_grad = (
        hidden_grad * up_act * sigmoid_gate * (1.0 + gate_act * (1.0 - sigmoid_gate))
    ).astype(jnp.bfloat16)
    up_grad = (hidden_grad * silu_gate).astype(jnp.bfloat16)
    return (gate_grad, up_grad)


def neighbour(**place):
    return {axis: place.get(axis, lax.axis_index(axis)) for axis in (*SEQ, "exp")}


ARRIVALS = (
    (0, 0, 0),
    (0, 0, 1),
    (0, 3, 0),
    (0, 1, 0),
    (1, 0, 0),
    (0, 2, 0),
    (0, 3, 1),
    (0, 1, 1),
    (1, 0, 1),
    (0, 2, 1),
    (1, 3, 0),
    (1, 1, 0),
    (1, 2, 0),
    (1, 3, 1),
    (1, 1, 1),
    (1, 2, 1),
)
PASS_TURNS = {
    (0, 3, 0): 2,
    (0, 1, 0): 2,
    (1, 0, 0): 4,
    (0, 2, 0): 4,
    (1, 3, 0): 10,
    (1, 1, 0): 11,
    (1, 2, 0): 12,
}
ODD_LAG = 2
WEIGHTS_START = 2
PUSH_START = 5
WEIGHTS_PASS = 11
WEIGHTS_LAST = 15


def attention_kernel(
    queries_ref,
    keyvals_ref,
    grads_ref,
    gate_ref,
    up_ref,
    heads_out,
    grads_out,
    weights_out,
    kv_all,
    odd_out,
    odd_in,
    turned,
    m_ref,
    acc_ref,
    mixed_ref,
    kv_send,
    kv_recv,
    odd_sem,
    push_send,
    push_recv,
    heads_send,
    heads_recv,
    weight_send,
    weight_recv,
    local_sem,
):
    zl, y, c, ex = (lax.axis_index(a) for a in (*SEQ, "exp"))
    half_rows = odd_in.shape[1]
    heads = odd_in.shape[0] // HEAD_DIM
    pieces = half_rows // 128
    experts = grads_ref.shape[0]
    shard = zl * 8 + y * 2 + c
    mirror = 15 - shard
    core_peer = neighbour(c=1 - c)
    z_peer = neighbour(zl=1 - zl)
    y_up = neighbour(y=lax.rem(y + 1, 4))
    y_down = neighbour(y=lax.rem(y + 3, 4))
    y_far = neighbour(y=lax.rem(y + 2, 4))

    def mirrored(e):
        return {"zl": 1 - zl, "y": 3 - y, "c": 1 - c, "exp": e}

    barrier = pltpu.get_barrier_semaphore()
    greeted = [core_peer, y_up, y_down, y_far]
    for d in range(experts):
        e = lax.rem(ex + d, experts)
        greeted += [mirrored(e), neighbour(zl=1 - zl, exp=e)]
        if d:
            greeted.append(neighbour(exp=e))
    for other in greeted:
        pl.semaphore_signal(barrier, inc=1, device_id=other, device_id_type=MESH)

    own_weights = [
        pltpu.make_async_copy(ref.at[0], weights_out.at[n, c, y], local_sem.at[n])
        for n, ref in enumerate((gate_ref, up_ref))
    ]
    own_grads = pltpu.make_async_copy(grads_ref.at[ex], grads_out.at[zl, ex], local_sem.at[3])
    for copy in (*own_weights, own_grads):
        copy.start()

    keyvals = keyvals_ref[...]
    kv_all[shard, pl.ds(0, half_rows), :] = jnp.concatenate(
        [keyvals[:half_rows, :HEAD_DIM], keyvals[half_rows:, :HEAD_DIM]], axis=1
    )
    values = keyvals.T[HEAD_DIM:]
    for p in range(2 * pieces):
        kv_all[shard, pl.ds(half_rows + p * HEAD_DIM, HEAD_DIM), :] = values[
            :, p * 128 : (p + 1) * 128
        ]

    def turn(half, flipped):
        flat = jnp.concatenate(
            [flipped[h * HEAD_DIM : (h + 1) * HEAD_DIM] for h in range(heads)], axis=1
        )
        empty = jnp.zeros_like(flat)
        turned[half, 0] = jnp.concatenate([flat, empty], axis=0)
        turned[half, 1] = jnp.concatenate([empty, flat], axis=0)

    odd_out[...] = queries_ref[pl.ds(half_rows, half_rows), :].T
    turn(0, queries_ref[pl.ds(0, half_rows), :].T)
    m_ref[...] = jnp.full_like(m_ref, very_negative)
    acc_ref[...] = jnp.zeros_like(acc_ref)
    pl.semaphore_wait(barrier, len(greeted))

    odd_copy = pltpu.make_async_remote_copy(
        src_ref=odd_out,
        dst_ref=odd_in,
        send_sem=odd_sem.at[0],
        recv_sem=odd_sem.at[1],
        device_id=mirrored(ex),
        device_id_type=MESH,
    )

    def shard_at(dz, dy, dc):
        return lax.rem(zl + dz, 2) * 8 + lax.rem(y + dy, 4) * 2 + lax.rem(c + dc, 2)

    def pass_on(index, t, to):
        return pltpu.make_async_remote_copy(
            src_ref=kv_all.at[t],
            dst_ref=kv_all.at[t],
            send_sem=kv_send.at[index],
            recv_sem=kv_recv.at[t],
            device_id=to,
            device_id_type=MESH,
        )

    routes = {
        (0, 0, 0): (z_peer, y_up, y_down, y_far, core_peer),
        (0, 3, 0): (z_peer, core_peer),
        (0, 1, 0): (z_peer, core_peer),
        (0, 2, 0): (z_peer, core_peer),
        (1, 0, 0): (core_peer,),
        (1, 3, 0): (core_peer,),
        (1, 1, 0): (core_peer,),
        (1, 2, 0): (core_peer,),
    }
    forwards = {}
    for place, targets in routes.items():
        first = sum(len(f) for f in forwards.values())
        forwards[place] = [
            pass_on(first + n, shard_at(*place), to) for n, to in enumerate(targets)
        ]

    def weight_copy(index, rows, dy, to, dc=0):
        part = weights_out.at[:, lax.rem(c + dc, 2), lax.rem(y + dy, 4), rows]
        return pltpu.make_async_remote_copy(
            src_ref=part,
            dst_ref=part,
            send_sem=weight_send.at[index],
            recv_sem=weight_recv.at[index],
            device_id=to,
            device_id_type=MESH,
        )

    owned = weights_out.shape[3]
    every, low, high = pl.ds(0, owned), pl.ds(0, owned // 2), pl.ds(owned // 2, owned // 2)
    weight_own = [
        weight_copy(0, every, 0, y_up),
        weight_copy(1, every, 0, y_down),
        weight_copy(2, every, 0, core_peer),
    ]
    weight_above = weight_copy(3, low, 3, y_up)
    weight_below = weight_copy(4, high, 1, y_down)
    weight_core = [
        weight_copy(5, every, 3, core_peer),
        weight_copy(6, every, 1, core_peer),
        weight_copy(7, every, 2, core_peer),
    ]

    pushes = []
    for index in range(1, 2 * experts):
        dz, de = divmod(index, experts)
        e = lax.rem(ex + de, experts)
        pushes.append(
            pltpu.make_async_remote_copy(
                src_ref=grads_ref.at[e],
                dst_ref=grads_out.at[zl, ex],
                send_sem=push_send.at[index],
                recv_sem=push_recv.at[index],
                device_id=neighbour(zl=lax.rem(zl + dz, 2), exp=e),
                device_id_type=MESH,
            )
        )

    odd_copy.start()
    for copy in forwards[(0, 0, 0)]:
        copy.start()

    ones = jnp.ones((16, half_rows), jnp.bfloat16)

    def values_of(block, part):
        turned_values = [
            kv_all[block, pl.ds(half_rows + (part * pieces + p) * HEAD_DIM, HEAD_DIM), :]
            for p in range(pieces)
        ]
        return jnp.concatenate([jnp.concatenate(turned_values, axis=1), ones], axis=0)

    def step(half, block, parts, masked):
        keys = kv_all[block, pl.ds(0, half_rows), :]
        scores = []
        for part in range(parts):
            s = (
                jnp.dot(keys, turned[half, part], preferred_element_type=jnp.float32)
                * score_to_log2
            )
            if masked and part == parts - 1:
                key_place = lax.broadcasted_iota(jnp.int32, s.shape, 0)
                query_place = lax.broadcasted_iota(jnp.int32, s.shape, 1) % half_rows
                s = jnp.where(key_place <= query_place, s, very_negative)
            scores.append(s)
        old = m_ref[half]
        new = old
        for s in scores:
            new = jnp.maximum(new, jnp.max(s, axis=0, keepdims=True))
        m_ref[half] = new
        total = acc_ref[half] * jnp.exp2(old - new)
        for part, s in enumerate(scores):
            weights = jnp.exp2(s - new).astype(jnp.bfloat16)
            total += jnp.dot(values_of(block, part), weights, preferred_element_type=jnp.float32)
        acc_ref[half] = total

    step(0, shard, 1, True)

    def slot_shard(slot):
        def pick(axis):
            return sum(
                jnp.where(slot == n, place[axis], 0) for n, place in enumerate(ARRIVALS)
            )

        return shard_at(pick(0), pick(1), pick(2))

    def visit(slot, carry):
        for n, place in enumerate(ARRIVALS):
            if place in PASS_TURNS:

                @pl.when(slot == PASS_TURNS[place])
                def _():
                    pass_on(0, shard_at(*place), core_peer).wait_recv()
                    for copy in forwards[place]:
                        copy.start()

            elif n:

                @pl.when(slot == n)
                def _():
                    pass_on(0, shard_at(*place), core_peer).wait_recv()

        @pl.when(slot == ODD_LAG)
        def _():
            odd_copy.wait_recv()
            turn(1, odd_in[...])

        @pl.when(slot == WEIGHTS_START)
        def _():
            for copy in own_weights:
                copy.wait()
            for copy in weight_own:
                copy.start()

        @pl.when(slot == PUSH_START)
        def _():
            for copy in pushes:
                copy.start()

        @pl.when(slot == WEIGHTS_PASS)
        def _():
            weight_own[0].wait_recv()
            weight_above.start()
            weight_core[0].start()
            weight_own[1].wait_recv()
            weight_below.start()
            weight_core[1].start()

        @pl.when(slot == WEIGHTS_LAST)
        def _():
            weight_above.wait_recv()
            weight_below.wait_recv()
            weight_core[2].start()

        def one_half(half, inner):
            seen = slot - ODD_LAG * half
            t = slot_shard(seen)
            here = (seen >= 0) & (seen < len(ARRIVALS))

            @pl.when(here & (t < jnp.where(half == 0, shard, mirror)))
            def _():
                step(half, t, 2, False)

            return inner

        lax.fori_loop(0, 2, one_half, 0)
        return carry

    lax.fori_loop(0, len(ARRIVALS) + ODD_LAG, visit, 0)
    step(1, mirror, 2, True)

    for half in range(2):
        total = acc_ref[half]
        mixed = total[:HEAD_DIM] / total[HEAD_DIM : HEAD_DIM + 1]
        for head in range(heads):
            for block in range(pieces):
                start = head * half_rows + block * 128
                mixed_ref[half, block, pl.ds(head * HEAD_DIM, HEAD_DIM), :] = mixed[
                    :, start : start + 128
                ].astype(jnp.bfloat16)

    def head_copy(half, block, to):
        return pltpu.make_async_remote_copy(
            src_ref=mixed_ref.at[half, block],
            dst_ref=heads_out.at[ex],
            send_sem=heads_send.at[half, block],
            recv_sem=heads_recv.at[ex],
            device_id=to,
            device_id_type=MESH,
        )

    even_copies = []
    for d in range(4):
        block = lax.rem(ex + d, 4)
        even_copies.append(head_copy(0, block, neighbour(exp=block)))
    odd_copies = []
    for d in range(4):
        block = lax.rem(ex + d, 4)
        odd_copies.append(head_copy(1, block, mirrored(4 + block)))
    own_heads = pltpu.make_async_copy(
        mixed_ref.at[0, lax.rem(ex, 4)], heads_out.at[ex], local_sem.at[4]
    )
    for copy in (*odd_copies, *even_copies[1:]):
        copy.start()

    @pl.when(ex < 4)
    def _():
        own_heads.start()

    @pl.when(ex >= 4)
    def _():
        even_copies[0].start()

    def head_arrival(e):
        return pltpu.make_async_remote_copy(
            src_ref=mixed_ref.at[0, 0],
            dst_ref=heads_out.at[e],
            send_sem=heads_send.at[0, 0],
            recv_sem=heads_recv.at[e],
            device_id=core_peer,
            device_id_type=MESH,
        )

    for d in range(1, experts):
        head_arrival(lax.rem(ex + d, experts)).wait_recv()

    @pl.when(ex < 4)
    def _():
        own_heads.wait()

    @pl.when(ex >= 4)
    def _():
        head_arrival(ex).wait_recv()
        even_copies[0].wait_send()

    own_grads.wait()
    for copy in pushes:
        copy.wait()
    weight_own[2].wait_recv()
    for copy in weight_core:
        copy.wait_recv()
    odd_copy.wait_send()
    for copies in forwards.values():
        for copy in copies:
            copy.wait_send()
    for copy in (*weight_own, weight_above, weight_below, *weight_core):
        copy.wait_send()
    for copy in (*odd_copies, *even_copies[1:]):
        copy.wait_send()


def attend(queries, keyvals, send_grads, w_gate, w_up):
    row_count, query_width = queries.shape
    half_rows = row_count // 2
    heads = query_width // HEAD_DIM
    experts, capacity, width = send_grads.shape
    owned = w_gate.shape[1]
    bf16 = jnp.bfloat16
    vmem = pl.BlockSpec(memory_space=pltpu.VMEM)
    anywhere = pl.BlockSpec(memory_space=pl.ANY)
    dma = pltpu.SemaphoreType.DMA
    return pl.pallas_call(
        attention_kernel,
        out_shape=(
            jax.ShapeDtypeStruct((experts, query_width, row_count // experts), bf16),
            jax.ShapeDtypeStruct((2, experts, capacity, width), bf16),
            jax.ShapeDtypeStruct((2, 2, 4, owned, width), bf16),
        ),
        in_specs=[vmem] * 2 + [anywhere] * 3,
        out_specs=(anywhere,) * 3,
        scratch_shapes=[
            pltpu.VMEM((len(ARRIVALS), row_count, 2 * HEAD_DIM), bf16),
            pltpu.VMEM((query_width, half_rows), bf16),
            pltpu.VMEM((query_width, half_rows), bf16),
            pltpu.VMEM((2, 2, 2 * HEAD_DIM, heads * half_rows), bf16),
            pltpu.VMEM((2, 1, heads * half_rows), jnp.float32),
            pltpu.VMEM((2, HEAD_DIM + 16, heads * half_rows), jnp.float32),
            pltpu.VMEM((2, half_rows // 128, query_width, 128), bf16),
            dma((15,)),
            dma((len(ARRIVALS),)),
            dma((2,)),
            dma((2 * experts,)),
            dma((2 * experts,)),
            dma((2, 4)),
            dma((experts,)),
            dma((8,)),
            dma((8,)),
            dma((5,)),
        ],
        compiler_params=pltpu.CompilerParams(
            collective_id=0, has_side_effects=True, vmem_limit_bytes=48 * 2**20
        ),
        cost_estimate=pl.CostEstimate(
            flops=20_000_000_000, bytes_accessed=20_000_000, transcendentals=27_000_000
        ),
        name="attention",
    )(queries, keyvals, send_grads, w_gate, w_up)


def expert_kernel(
    rows_ref,
    cot_in,
    weights_ref,
    own_down_ref,
    hidden_ref,
    combine_ref,
    layer_ref,
    grad_gate_ref,
    grad_up_ref,
    grad_down_ref,
    rows_in,
    down_in,
    out_buf,
    out_in,
    parts,
    core_in,
    sums,
    half_up_in,
    half_down_in,
    full_up_in,
    full_down_in,
    push_send,
    push_recv,
    ring_send,
    ring_recv,
    weight_send,
    weight_recv,
    local_sem,
):
    zl, y, c, ex = (lax.axis_index(a) for a in (*SEQ, "exp"))
    experts = rows_ref.shape[0]
    capacity, width = rows_ref.shape[1:]
    tokens = 2 * experts * capacity
    core_peer = neighbour(c=1 - c)
    y_up = neighbour(y=lax.rem(y + 1, 4))
    y_down = neighbour(y=lax.rem(y + 3, 4))
    offsets = [(dz, de) for dz in range(2) for de in range(experts)]

    def peer(dz, de):
        return lax.rem(zl + dz, 2), lax.rem(ex + de, experts)

    def source(dz, de):
        return lax.rem(zl + 2 - dz, 2), lax.rem(ex + experts - de, experts)

    down_in[c, y] = own_down_ref[0]
    barrier = pltpu.get_barrier_semaphore()
    for dz, de in offsets[1:]:
        tz, te = peer(dz, de)
        pl.semaphore_signal(
            barrier, inc=1, device_id=neighbour(zl=tz, exp=te), device_id_type=MESH
        )
    for other in (core_peer, y_up, y_down):
        pl.semaphore_signal(barrier, inc=1, device_id=other, device_id_type=MESH)
    pl.semaphore_wait(barrier, len(offsets) + 2)

    def push(kind, index, src, dst, to):
        return pltpu.make_async_remote_copy(
            src_ref=src,
            dst_ref=dst,
            send_sem=push_send.at[kind, index],
            recv_sem=push_recv.at[kind, index],
            device_id=to,
            device_id_type=MESH,
        )

    def spread(kind, src_ref, dst_ref):
        own = pltpu.make_async_copy(src_ref.at[ex], dst_ref.at[zl, ex], local_sem.at[kind])
        own.start()
        sent = []
        for index, (dz, de) in enumerate(offsets):
            if index:
                tz, te = peer(dz, de)
                copy = push(
                    kind, index, src_ref.at[te], dst_ref.at[zl, ex], neighbour(zl=tz, exp=te)
                )
                copy.start()
                sent.append(copy)
        return own, sent

    def arrive(spread_copies):
        own, sent = spread_copies
        own.wait()
        for copy in sent:
            copy.wait_recv()

    rows_copies = spread(1, rows_ref, rows_in)

    def flat(ref):
        return ref[...].reshape(tokens, width)

    def ring(mat, stage, src, dst, to):
        return pltpu.make_async_remote_copy(
            src_ref=src,
            dst_ref=dst,
            send_sem=ring_send.at[mat, stage],
            recv_sem=ring_recv.at[mat, stage],
            device_id=to,
            device_id_type=MESH,
        )

    chunk = 512

    def partial(mat, first, second):
        turned = first.T
        for start in range(0, width, chunk):
            part = jnp.dot(
                turned, second[:, start : start + chunk], preferred_element_type=jnp.float32
            ).astype(jnp.bfloat16)
            parts[mat, :, :, :, pl.ds(start, chunk)] = part.reshape(2, 4, -1, chunk)

    started = []

    def go(copy):
        copy.start()
        started.append(copy)
        return copy

    def core_stage(mat):
        return go(ring(mat, 0, parts.at[mat, 1 - c], core_in.at[mat], core_peer))

    def wide(value):
        return value.astype(jnp.float32)

    half = parts.shape[3] // 2

    def half_stage(mat, core_copy):
        core_copy.wait_recv()
        sums[mat] = (wide(parts[mat, c]) + wide(core_in[mat])).astype(jnp.bfloat16)
        far = lax.rem(y + 2, 4)
        return (
            go(ring(mat, 1, sums.at[mat, far, pl.ds(0, half)], half_up_in.at[mat], y_up)),
            go(ring(mat, 2, sums.at[mat, far, pl.ds(half, half)], half_down_in.at[mat], y_down)),
        )

    def full_stage(mat, copies):
        above = lax.rem(y + 1, 4)
        below = lax.rem(y + 3, 4)
        copies[0].wait_recv()
        low = pl.ds(0, half)
        sums[mat, above, low] = (wide(sums[mat, above, low]) + wide(half_up_in[mat])).astype(
            jnp.bfloat16
        )
        first = go(ring(mat, 3, sums.at[mat, above], full_up_in.at[mat], y_up))
        copies[1].wait_recv()
        high = pl.ds(half, half)
        sums[mat, below, high] = (wide(sums[mat, below, high]) + wide(half_down_in[mat])).astype(
            jnp.bfloat16
        )
        return (first, go(ring(mat, 4, sums.at[mat, below], full_down_in.at[mat], y_down)))

    def finish(mat, copies, out_ref):
        for copy in copies:
            copy.wait_recv()
        out_ref[0] = (wide(sums[mat, y]) + wide(full_up_in[mat]) + wide(full_down_in[mat])).astype(
            jnp.bfloat16
        )

    def weight_copy(index, rows, dy, to):
        part = down_in.at[c, lax.rem(y + dy, 4), rows]
        return pltpu.make_async_remote_copy(
            src_ref=part,
            dst_ref=part,
            send_sem=weight_send.at[index],
            recv_sem=weight_recv.at[index],
            device_id=to,
            device_id_type=MESH,
        )

    owned = down_in.shape[2]
    every, low, high = pl.ds(0, owned), pl.ds(0, owned // 2), pl.ds(owned // 2, owned // 2)
    weight_own = [
        go(weight_copy(0, every, 0, y_up)),
        go(weight_copy(1, every, 0, y_down)),
        go(weight_copy(2, every, 0, core_peer)),
    ]
    weight_own[0].wait_recv()
    weight_above = go(weight_copy(3, low, 3, y_up))
    weight_core = [go(weight_copy(5, every, 3, core_peer))]
    weight_own[1].wait_recv()
    weight_below = go(weight_copy(4, high, 1, y_down))
    weight_core.append(go(weight_copy(6, every, 1, core_peer)))
    weight_above.wait_recv()
    weight_below.wait_recv()
    weight_core.append(go(weight_copy(7, every, 2, core_peer)))
    for copy in (weight_own[2], *weight_core):
        copy.wait_recv()
    gate, up = (weights_ref[n].reshape(-1, width) for n in range(2))
    down = down_in[...].reshape(-1, width)
    output_grads = flat(cot_in)
    hidden_grad = contract_cols(output_grads, down)
    arrive(rows_copies)
    expert_rows = flat(rows_in)
    gate_act = contract_cols(expert_rows, gate)
    up_act = contract_cols(expert_rows, up)
    hidden_units = swiglu_forward(gate_act, up_act)
    partial(0, hidden_units, output_grads)
    core_down = core_stage(0)
    gate_grad, up_grad = swiglu_backward(gate_act, up_act, hidden_grad)
    partial(1, gate_grad, expert_rows)
    core_gate = core_stage(1)
    half_down = half_stage(0, core_down)
    partial(2, up_grad, expert_rows)
    core_up = core_stage(2)
    half_gate = half_stage(1, core_gate)
    for start in range(0, width, chunk):
        out_buf[:, :, :, pl.ds(start, chunk)] = (
            jnp.dot(
                hidden_units,
                down[:, start : start + chunk],
                preferred_element_type=jnp.float32,
            )
            .astype(jnp.bfloat16)
            .reshape(2, experts, capacity, chunk)
        )
    own_out = pltpu.make_async_copy(out_buf.at[zl, ex], out_in.at[zl, ex], local_sem.at[2])
    own_out.start()
    back = []
    for index, (dz, de) in enumerate(offsets):
        if index:
            tz, te = peer(dz, de)
            copy = push(
                2, index, out_buf.at[tz, te], out_in.at[zl, ex], neighbour(zl=tz, exp=te)
            )
            copy.start()
            back.append(copy)
    full_down = full_stage(0, half_down)
    half_up = half_stage(2, core_up)
    full_gate = full_stage(1, half_gate)
    full_up = full_stage(2, half_up)
    finish(0, full_down, grad_down_ref)
    arrive((own_out, back))
    for start in range(0, width, chunk):
        cols = pl.ds(start, chunk)
        returned = out_in[:, :, :, cols].reshape(tokens, chunk)
        layer_ref[:, cols] = (
            wide(hidden_ref[:, cols])
            + jnp.dot(combine_ref[...], returned, preferred_element_type=jnp.float32)
        ).astype(jnp.bfloat16)
    finish(1, full_gate, grad_gate_ref)
    finish(2, full_up, grad_up_ref)
    for copy in (*rows_copies[1], *back, *started):
        copy.wait_send()


def expert_layer(send_rows, grad_rows, weights, w_down, hidden_state, dispatch_table):
    experts, capacity, width = send_rows.shape
    owned = weights.shape[3]
    token_count = hidden_state.shape[0]
    combine = jnp.concatenate([dispatch_table, dispatch_table], axis=0).T
    vmem = pl.BlockSpec(memory_space=pltpu.VMEM)
    bf16 = jnp.bfloat16
    landing = pltpu.VMEM((2, experts, capacity, width), bf16)
    grad_shape = jax.ShapeDtypeStruct((1, owned, width), bf16)
    return pl.pallas_call(
        expert_kernel,
        out_shape=(jax.ShapeDtypeStruct((token_count, width), bf16),) + (grad_shape,) * 3,
        in_specs=[vmem] * 6,
        out_specs=(vmem,) * 4,
        scratch_shapes=[
            landing,
            pltpu.VMEM((2, 4, owned, width), bf16),
            landing,
            landing,
            pltpu.VMEM((3, 2, 4, owned, width), bf16),
            pltpu.VMEM((3, 4, owned, width), bf16),
            pltpu.VMEM((3, 4, owned, width), bf16),
            pltpu.VMEM((3, owned // 2, width), bf16),
            pltpu.VMEM((3, owned // 2, width), bf16),
            pltpu.VMEM((3, owned, width), bf16),
            pltpu.VMEM((3, owned, width), bf16),
            pltpu.SemaphoreType.DMA((3, 2 * experts)),
            pltpu.SemaphoreType.DMA((3, 2 * experts)),
            pltpu.SemaphoreType.DMA((3, 5)),
            pltpu.SemaphoreType.DMA((3, 5)),
            pltpu.SemaphoreType.DMA((8,)),
            pltpu.SemaphoreType.DMA((8,)),
            pltpu.SemaphoreType.DMA((3,)),
        ],
        compiler_params=pltpu.CompilerParams(
            collective_id=1, has_side_effects=True, vmem_limit_bytes=56 * 2**20
        ),
        cost_estimate=pl.CostEstimate(
            flops=5_000_000_000, bytes_accessed=20_000_000, transcendentals=200_000
        ),
        name="experts",
    )(send_rows, grad_rows, weights, w_down, hidden_state, combine)


def local(
    resid,
    queries,
    keyvals,
    out_proj,
    norm_gain,
    token_ids,
    hash_table,
    w_gate,
    w_up,
    w_down,
    cotangent,
):
    token_count = resid.shape[0]
    model_width = resid.shape[1]
    expert_count = lax.axis_size("exp")
    capacity = token_count // expert_count
    expert_of = jnp.take(hash_table, token_ids)
    onehot_slots = (
        expert_of[:, None] == jnp.arange(expert_count, dtype=jnp.int32)[None, :]
    ).astype(jnp.int32)
    earlier = jnp.cumsum(onehot_slots, axis=0) - onehot_slots
    slot_of = jnp.sum(onehot_slots * earlier, axis=1)
    target = jnp.where(slot_of < capacity, expert_of * capacity + slot_of, -1)
    dispatch_table = (
        jnp.arange(expert_count * capacity, dtype=jnp.int32)[:, None] == target[None, :]
    ).astype(jnp.bfloat16)

    def placed(rows):
        return (
            jnp.dot(dispatch_table, rows, preferred_element_type=jnp.float32)
            .astype(jnp.bfloat16)
            .reshape(expert_count, capacity, model_width)
        )

    token_heads, grad_rows, weights = attend(
        queries, keyvals, placed(cotangent), w_gate, w_up
    )
    projected = contract_rows(token_heads.reshape(-1, token_count), out_proj)
    hidden_state = (resid.astype(jnp.float32) + projected).astype(jnp.bfloat16)
    widened = hidden_state.astype(jnp.float32)
    mean_square = jnp.mean(widened * widened, axis=1, keepdims=True)
    normed = (widened * lax.rsqrt(mean_square + norm_eps) * norm_gain.astype(jnp.float32)).astype(
        jnp.bfloat16
    )
    return expert_layer(
        placed(normed), grad_rows, weights, w_down, hidden_state, dispatch_table
    )


def solution(mesh):
    fine_mesh = Mesh(mesh.devices.reshape(2, 4, 2, 8), ("zl", "y", "c", "exp"))
    token_spec = P((*SEQ, "exp"), None)
    weight_spec = P("exp", SEQ, None)
    in_specs = (
        token_spec,
        P(SEQ, "exp"),
        P(SEQ, "exp"),
        P(),
        P(),
        P((*SEQ, "exp")),
        P(),
        weight_spec,
        weight_spec,
        weight_spec,
        token_spec,
    )
    out_specs = (token_spec, weight_spec, weight_spec, weight_spec)
    return jax.shard_map(
        local, mesh=fine_mesh, in_specs=in_specs, out_specs=out_specs, check_vma=False
    )
```

```python
import functools
import math

import jax
import jax.numpy as jnp
from jax import lax
from jax.experimental import pallas as pl
from jax.experimental.pallas import tpu as pltpu
from jax.sharding import Mesh
from jax.sharding import PartitionSpec as P

HEAD_DIM = 64
SEQ = ("zl", "y", "c")
MESH = pl.DeviceIdType.MESH
score_to_log2 = math.log2(math.e) / math.sqrt(HEAD_DIM)
very_negative = -1e30
norm_eps = 1e-05


def contract_rows(first_operand, second_operand):
    return lax.dot_general(
        first_operand, second_operand, (((0,), (0,)), ((), ())), preferred_element_type=jnp.float32
    )


def contract_cols(first_operand, second_operand):
    return lax.dot_general(
        first_operand, second_operand, (((1,), (1,)), ((), ())), preferred_element_type=jnp.float32
    )


def swiglu_forward(gate_act, up_act):
    sigmoid_gate = jax.nn.sigmoid(gate_act)
    silu_gate = gate_act * sigmoid_gate
    return (silu_gate * up_act).astype(jnp.bfloat16)


def swiglu_backward(gate_act, up_act, hidden_grad):
    sigmoid_gate = jax.nn.sigmoid(gate_act)
    silu_gate = gate_act * sigmoid_gate
    gate_grad = (
        hidden_grad * up_act * sigmoid_gate * (1.0 + gate_act * (1.0 - sigmoid_gate))
    ).astype(jnp.bfloat16)
    up_grad = (hidden_grad * silu_gate).astype(jnp.bfloat16)
    return (gate_grad, up_grad)


def neighbour(**place):
    return {axis: place.get(axis, lax.axis_index(axis)) for axis in (*SEQ, "exp")}


ARRIVALS = (
    (0, 0, 0),
    (0, 0, 1),
    (0, 3, 0),
    (0, 1, 0),
    (1, 0, 0),
    (0, 2, 0),
    (0, 3, 1),
    (0, 1, 1),
    (1, 0, 1),
    (1, 3, 0),
    (1, 1, 0),
    (1, 2, 0),
    (0, 2, 1),
    (1, 3, 1),
    (1, 1, 1),
    (1, 2, 1),
)
PASS_TURNS = {
    (0, 3, 0): 2,
    (0, 1, 0): 2,
    (1, 0, 0): 4,
    (0, 2, 0): 5,
    (1, 3, 0): 7,
    (1, 1, 0): 8,
    (1, 2, 0): 8,
}
KEY_PIECE = 256
ODD_LAG = 2
FAR_START = 2
WEIGHTS_START = 4
PUSH_START = 9
WEIGHTS_PASS = 14
WEIGHTS_LAST = 17


def attention_kernel(
    queries_ref,
    keyvals_ref,
    grads_ref,
    gate_ref,
    up_ref,
    heads_out,
    grads_out,
    weights_out,
    kv_all,
    odd_out,
    odd_in,
    turned,
    m_ref,
    peak_ref,
    scores_ref,
    acc_ref,
    mixed_ref,
    kv_send,
    kv_recv,
    odd_sem,
    push_send,
    push_recv,
    heads_send,
    heads_recv,
    weight_send,
    weight_recv,
    local_sem,
):
    zl, y, c, ex = (lax.axis_index(a) for a in (*SEQ, "exp"))
    half_rows = odd_in.shape[1]
    heads = odd_in.shape[0] // HEAD_DIM
    pieces = half_rows // 128
    experts = grads_ref.shape[0]
    shard = zl * 8 + y * 2 + c
    mirror = 15 - shard
    core_peer = neighbour(c=1 - c)
    z_peer = neighbour(zl=1 - zl)
    y_up = neighbour(y=lax.rem(y + 1, 4))
    y_down = neighbour(y=lax.rem(y + 3, 4))
    y_far = neighbour(y=lax.rem(y + 2, 4))

    def mirrored(e):
        return {"zl": 1 - zl, "y": 3 - y, "c": 1 - c, "exp": e}

    barrier = pltpu.get_barrier_semaphore()
    greeted = [core_peer, y_up, y_down, y_far]
    for d in range(experts):
        e = lax.rem(ex + d, experts)
        greeted += [mirrored(e), neighbour(zl=1 - zl, exp=e)]
        if d:
            greeted.append(neighbour(exp=e))
    for other in greeted:
        pl.semaphore_signal(barrier, inc=1, device_id=other, device_id_type=MESH)

    own_weights = [
        pltpu.make_async_copy(ref.at[0], weights_out.at[n, c, y], local_sem.at[n])
        for n, ref in enumerate((gate_ref, up_ref))
    ]
    own_grads = pltpu.make_async_copy(grads_ref.at[ex], grads_out.at[zl, ex], local_sem.at[3])
    for copy in (*own_weights, own_grads):
        copy.start()

    keyvals = keyvals_ref[...]
    kv_all[shard, pl.ds(0, half_rows), :] = jnp.concatenate(
        [keyvals[:half_rows, :HEAD_DIM], keyvals[half_rows:, :HEAD_DIM]], axis=1
    )
    values = keyvals.T[HEAD_DIM:]
    for p in range(2 * pieces):
        kv_all[shard, pl.ds(half_rows + p * HEAD_DIM, HEAD_DIM), :] = values[
            :, p * 128 : (p + 1) * 128
        ]

    def turn(half, flipped):
        flat = jnp.concatenate(
            [flipped[h * HEAD_DIM : (h + 1) * HEAD_DIM] for h in range(heads)], axis=1
        )
        empty = jnp.zeros_like(flat)
        turned[half, 0] = jnp.concatenate([flat, empty], axis=0)
        turned[half, 1] = jnp.concatenate([empty, flat], axis=0)

    odd_out[...] = queries_ref[pl.ds(half_rows, half_rows), :].T
    turn(0, queries_ref[pl.ds(0, half_rows), :].T)
    m_ref[...] = jnp.full_like(m_ref, very_negative)
    acc_ref[...] = jnp.zeros_like(acc_ref)
    pl.semaphore_wait(barrier, len(greeted))

    odd_copy = pltpu.make_async_remote_copy(
        src_ref=odd_out,
        dst_ref=odd_in,
        send_sem=odd_sem.at[0],
        recv_sem=odd_sem.at[1],
        device_id=mirrored(ex),
        device_id_type=MESH,
    )

    def shard_at(dz, dy, dc):
        return lax.rem(zl + dz, 2) * 8 + lax.rem(y + dy, 4) * 2 + lax.rem(c + dc, 2)

    def pass_on(index, t, to):
        return pltpu.make_async_remote_copy(
            src_ref=kv_all.at[t],
            dst_ref=kv_all.at[t],
            send_sem=kv_send.at[index],
            recv_sem=kv_recv.at[t],
            device_id=to,
            device_id_type=MESH,
        )

    routes = {
        (0, 0, 0): (z_peer, y_up, y_down, core_peer, y_far),
        (0, 3, 0): (z_peer, core_peer),
        (0, 1, 0): (z_peer, core_peer),
        (1, 0, 0): (y_far, core_peer),
        (0, 2, 0): (core_peer,),
        (1, 3, 0): (core_peer,),
        (1, 1, 0): (core_peer,),
        (1, 2, 0): (core_peer,),
    }
    forwards = {}
    for place, targets in routes.items():
        first = sum(len(f) for f in forwards.values())
        forwards[place] = [
            pass_on(first + n, shard_at(*place), to) for n, to in enumerate(targets)
        ]

    def weight_copy(index, rows, dy, to, dc=0):
        part = weights_out.at[:, lax.rem(c + dc, 2), lax.rem(y + dy, 4), rows]
        return pltpu.make_async_remote_copy(
            src_ref=part,
            dst_ref=part,
            send_sem=weight_send.at[index],
            recv_sem=weight_recv.at[index],
            device_id=to,
            device_id_type=MESH,
        )

    owned = weights_out.shape[3]
    every, low, high = pl.ds(0, owned), pl.ds(0, owned // 2), pl.ds(owned // 2, owned // 2)
    weight_own = [
        weight_copy(0, every, 0, y_up),
        weight_copy(1, every, 0, y_down),
        weight_copy(2, every, 0, core_peer),
    ]
    weight_above = weight_copy(3, low, 3, y_up)
    weight_below = weight_copy(4, high, 1, y_down)
    weight_core = [
        weight_copy(5, every, 3, core_peer),
        weight_copy(6, every, 1, core_peer),
        weight_copy(7, every, 2, core_peer),
    ]

    pushes = []
    for index in range(1, 2 * experts):
        dz, de = divmod(index, experts)
        e = lax.rem(ex + de, experts)
        pushes.append(
            pltpu.make_async_remote_copy(
                src_ref=grads_ref.at[e],
                dst_ref=grads_out.at[zl, ex],
                send_sem=push_send.at[index],
                recv_sem=push_recv.at[index],
                device_id=neighbour(zl=lax.rem(zl + dz, 2), exp=e),
                device_id_type=MESH,
            )
        )

    odd_copy.start()
    for copy in forwards[(0, 0, 0)][:4]:
        copy.start()

    ones = jnp.ones((16, half_rows), jnp.bfloat16)

    def values_of(block, part):
        turned_values = [
            kv_all[block, pl.ds(half_rows + (part * pieces + p) * HEAD_DIM, HEAD_DIM), :]
            for p in range(pieces)
        ]
        return jnp.concatenate([jnp.concatenate(turned_values, axis=1), ones], axis=0)

    def columns(head):
        return slice(head * half_rows, (head + 1) * half_rows)

    key_pieces = [pl.ds(start, KEY_PIECE) for start in range(0, half_rows, KEY_PIECE)]

    def score(half, block, part, rows, head, masked):
        s = (
            jnp.dot(
                kv_all[block, rows, :],
                turned[half, part, :, columns(head)],
                preferred_element_type=jnp.float32,
            )
            * score_to_log2
        )
        if masked:
            key_place = rows.start + lax.broadcasted_iota(jnp.int32, s.shape, 0)
            query_place = lax.broadcasted_iota(jnp.int32, s.shape, 1)
            s = jnp.where(key_place <= query_place, s, very_negative)
        return s

    def stage(slot, half, block, following=None):
        new = peak_ref[...]
        shrink = jnp.exp2(m_ref[half] - new)
        m_ref[half] = new
        if following is not None:
            next_half, next_block, masked = following
            start = m_ref[next_half]
        for head in range(heads):
            cols = columns(head)
            total = acc_ref[half, :, cols] * shrink[:, cols]
            if following is not None:
                peak = start[:, cols]
            for part in range(2):
                values = values_of(block, part)
                for rows in key_pieces:
                    if following is not None:
                        s = score(next_half, next_block, part, rows, head, masked and part == 1)
                        scores_ref[1 - slot, part, rows, cols] = s
                        peak = jnp.maximum(peak, jnp.max(s, axis=0, keepdims=True))
                    weights = jnp.exp2(scores_ref[slot, part, rows, cols] - new[:, cols])
                    total += jnp.dot(
                        values[:, rows.start : rows.start + KEY_PIECE],
                        weights.astype(jnp.bfloat16),
                        preferred_element_type=jnp.float32,
                    )
            acc_ref[half, :, cols] = total
            if following is not None:
                peak_ref[:, cols] = peak

    for head in range(heads):
        cols = columns(head)
        peak = m_ref[0, :, cols]
        for rows in key_pieces:
            s = score(0, shard, 0, rows, head, True)
            scores_ref[0, 0, rows, cols] = s
            scores_ref[0, 1, rows, cols] = jnp.full_like(s, very_negative)
            peak = jnp.maximum(peak, jnp.max(s, axis=0, keepdims=True))
        peak_ref[:, cols] = peak

    def slot_shard(slot):
        def pick(axis):
            return sum(
                jnp.where(slot == n, place[axis], 0) for n, place in enumerate(ARRIVALS)
            )

        return shard_at(pick(0), pick(1), pick(2))

    def visit(slot, carry):
        for n, place in enumerate(ARRIVALS):
            if place in PASS_TURNS:

                @pl.when(slot == PASS_TURNS[place])
                def _():
                    pass_on(0, shard_at(*place), core_peer).wait_recv()
                    for copy in forwards[place]:
                        copy.start()

            elif n:

                @pl.when(slot == n)
                def _():
                    pass_on(0, shard_at(*place), core_peer).wait_recv()

        @pl.when(slot == FAR_START)
        def _():
            forwards[(0, 0, 0)][4].start()

        @pl.when(slot == ODD_LAG)
        def _():
            odd_copy.wait_recv()
            turn(1, odd_in[...])

        @pl.when(slot == WEIGHTS_START)
        def _():
            for copy in own_weights:
                copy.wait()
            for copy in weight_own:
                copy.start()

        @pl.when(slot == PUSH_START)
        def _():
            for copy in pushes:
                copy.start()

        @pl.when(slot == WEIGHTS_PASS)
        def _():
            weight_own[0].wait_recv()
            weight_above.start()
            weight_core[0].start()
            weight_own[1].wait_recv()
            weight_below.start()
            weight_core[1].start()

        @pl.when(slot == WEIGHTS_LAST)
        def _():
            weight_above.wait_recv()
            weight_below.wait_recv()
            weight_core[2].start()

        def one_half(half, inner):
            last_half, last_block, scored = inner
            seen = slot - ODD_LAG * half
            t = slot_shard(seen)
            here = (seen >= 0) & (seen < len(ARRIVALS))

            used = here & (t < jnp.where(half == 0, shard, mirror))
            for now in range(2):

                @pl.when(used & (scored == now))
                def _():
                    stage(now, last_half, last_block, (half, t, False))

            return (
                jnp.where(used, half, last_half),
                jnp.where(used, t, last_block),
                jnp.where(used, 1 - scored, scored),
            )

        return lax.fori_loop(0, 2, one_half, carry)

    last_half, last_block, _ = lax.fori_loop(
        0, len(ARRIVALS) + ODD_LAG, visit, (jnp.int32(0), shard, jnp.int32(0))
    )
    stage(1, last_half, last_block, (1, mirror, True))
    stage(0, 1, mirror)

    for half in range(2):
        total = acc_ref[half]
        mixed = total[:HEAD_DIM] / total[HEAD_DIM : HEAD_DIM + 1]
        for head in range(heads):
            for block in range(pieces):
                start = head * half_rows + block * 128
                mixed_ref[half, block, pl.ds(head * HEAD_DIM, HEAD_DIM), :] = mixed[
                    :, start : start + 128
                ].astype(jnp.bfloat16)

    def head_copy(half, block, to):
        return pltpu.make_async_remote_copy(
            src_ref=mixed_ref.at[half, block],
            dst_ref=heads_out.at[ex],
            send_sem=heads_send.at[half, block],
            recv_sem=heads_recv.at[ex],
            device_id=to,
            device_id_type=MESH,
        )

    even_copies = []
    for d in range(4):
        block = lax.rem(ex + d, 4)
        even_copies.append(head_copy(0, block, neighbour(exp=block)))
    odd_copies = []
    for d in range(4):
        block = lax.rem(ex + d, 4)
        odd_copies.append(head_copy(1, block, mirrored(4 + block)))
    own_heads = pltpu.make_async_copy(
        mixed_ref.at[0, lax.rem(ex, 4)], heads_out.at[ex], local_sem.at[4]
    )
    for copy in (*odd_copies, *even_copies[1:]):
        copy.start()

    @pl.when(ex < 4)
    def _():
        own_heads.start()

    @pl.when(ex >= 4)
    def _():
        even_copies[0].start()

    def head_arrival(e):
        return pltpu.make_async_remote_copy(
            src_ref=mixed_ref.at[0, 0],
            dst_ref=heads_out.at[e],
            send_sem=heads_send.at[0, 0],
            recv_sem=heads_recv.at[e],
            device_id=core_peer,
            device_id_type=MESH,
        )

    for d in range(1, experts):
        head_arrival(lax.rem(ex + d, experts)).wait_recv()

    @pl.when(ex < 4)
    def _():
        own_heads.wait()

    @pl.when(ex >= 4)
    def _():
        head_arrival(ex).wait_recv()
        even_copies[0].wait_send()

    own_grads.wait()
    for copy in pushes:
        copy.wait()
    weight_own[2].wait_recv()
    for copy in weight_core:
        copy.wait_recv()
    odd_copy.wait_send()
    for copies in forwards.values():
        for copy in copies:
            copy.wait_send()
    for copy in (*weight_own, weight_above, weight_below, *weight_core):
        copy.wait_send()
    for copy in (*odd_copies, *even_copies[1:]):
        copy.wait_send()


def attend(queries, keyvals, send_grads, w_gate, w_up):
    row_count, query_width = queries.shape
    half_rows = row_count // 2
    heads = query_width // HEAD_DIM
    experts, capacity, width = send_grads.shape
    owned = w_gate.shape[1]
    bf16 = jnp.bfloat16
    vmem = pl.BlockSpec(memory_space=pltpu.VMEM)
    anywhere = pl.BlockSpec(memory_space=pl.ANY)
    dma = pltpu.SemaphoreType.DMA
    return pl.pallas_call(
        attention_kernel,
        out_shape=(
            jax.ShapeDtypeStruct((experts, query_width, row_count // experts), bf16),
            jax.ShapeDtypeStruct((2, experts, capacity, width), bf16),
            jax.ShapeDtypeStruct((2, 2, 4, owned, width), bf16),
        ),
        in_specs=[vmem] * 2 + [anywhere] * 3,
        out_specs=(anywhere,) * 3,
        scratch_shapes=[
            pltpu.VMEM((len(ARRIVALS), row_count, 2 * HEAD_DIM), bf16),
            pltpu.VMEM((query_width, half_rows), bf16),
            pltpu.VMEM((query_width, half_rows), bf16),
            pltpu.VMEM((2, 2, 2 * HEAD_DIM, heads * half_rows), bf16),
            pltpu.VMEM((2, 1, heads * half_rows), jnp.float32),
            pltpu.VMEM((1, heads * half_rows), jnp.float32),
            pltpu.VMEM((2, 2, half_rows, heads * half_rows), jnp.float32),
            pltpu.VMEM((2, HEAD_DIM + 16, heads * half_rows), jnp.float32),
            pltpu.VMEM((2, half_rows // 128, query_width, 128), bf16),
            dma((15,)),
            dma((len(ARRIVALS),)),
            dma((2,)),
            dma((2 * experts,)),
            dma((2 * experts,)),
            dma((2, 4)),
            dma((experts,)),
            dma((8,)),
            dma((8,)),
            dma((5,)),
        ],
        compiler_params=pltpu.CompilerParams(
            collective_id=0, has_side_effects=True, vmem_limit_bytes=48 * 2**20
        ),
        cost_estimate=pl.CostEstimate(
            flops=20_000_000_000, bytes_accessed=20_000_000, transcendentals=27_000_000
        ),
        name="attention",
    )(queries, keyvals, send_grads, w_gate, w_up)


def expert_kernel(
    rows_ref,
    cot_in,
    weights_ref,
    own_down_ref,
    hidden_ref,
    combine_ref,
    layer_ref,
    grad_gate_ref,
    grad_up_ref,
    grad_down_ref,
    rows_in,
    down_in,
    out_buf,
    out_in,
    parts,
    core_in,
    sums,
    half_up_in,
    half_down_in,
    full_up_in,
    full_down_in,
    push_send,
    push_recv,
    ring_send,
    ring_recv,
    weight_send,
    weight_recv,
    local_sem,
):
    zl, y, c, ex = (lax.axis_index(a) for a in (*SEQ, "exp"))
    experts = rows_ref.shape[0]
    capacity, width = rows_ref.shape[1:]
    tokens = 2 * experts * capacity
    core_peer = neighbour(c=1 - c)
    y_up = neighbour(y=lax.rem(y + 1, 4))
    y_down = neighbour(y=lax.rem(y + 3, 4))
    offsets = [(dz, de) for dz in range(2) for de in range(experts)]

    def peer(dz, de):
        return lax.rem(zl + dz, 2), lax.rem(ex + de, experts)

    def source(dz, de):
        return lax.rem(zl + 2 - dz, 2), lax.rem(ex + experts - de, experts)

    down_in[c, y] = own_down_ref[0]
    barrier = pltpu.get_barrier_semaphore()
    for dz, de in offsets[1:]:
        tz, te = peer(dz, de)
        pl.semaphore_signal(
            barrier, inc=1, device_id=neighbour(zl=tz, exp=te), device_id_type=MESH
        )
    for other in (core_peer, y_up, y_down):
        pl.semaphore_signal(barrier, inc=1, device_id=other, device_id_type=MESH)
    pl.semaphore_wait(barrier, len(offsets) + 2)

    def push(kind, index, src, dst, to):
        return pltpu.make_async_remote_copy(
            src_ref=src,
            dst_ref=dst,
            send_sem=push_send.at[kind, index],
            recv_sem=push_recv.at[kind, index],
            device_id=to,
            device_id_type=MESH,
        )

    def spread(kind, src_ref, dst_ref):
        own = pltpu.make_async_copy(src_ref.at[ex], dst_ref.at[zl, ex], local_sem.at[kind])
        own.start()
        sent = []
        for index, (dz, de) in enumerate(offsets):
            if index:
                tz, te = peer(dz, de)
                copy = push(
                    kind, index, src_ref.at[te], dst_ref.at[zl, ex], neighbour(zl=tz, exp=te)
                )
                copy.start()
                sent.append(copy)
        return own, sent

    def arrive(spread_copies):
        own, sent = spread_copies
        own.wait()
        for copy in sent:
            copy.wait_recv()

    rows_copies = spread(1, rows_ref, rows_in)

    def flat(ref):
        return ref[...].reshape(tokens, width)

    def ring(mat, stage, src, dst, to):
        return pltpu.make_async_remote_copy(
            src_ref=src,
            dst_ref=dst,
            send_sem=ring_send.at[mat, stage],
            recv_sem=ring_recv.at[mat, stage],
            device_id=to,
            device_id_type=MESH,
        )

    chunk = 512

    def partial(mat, first, second):
        turned = first.T
        for start in range(0, width, chunk):
            part = jnp.dot(
                turned, second[:, start : start + chunk], preferred_element_type=jnp.float32
            ).astype(jnp.bfloat16)
            parts[mat, :, :, :, pl.ds(start, chunk)] = part.reshape(2, 4, -1, chunk)

    started = []

    def go(copy):
        copy.start()
        started.append(copy)
        return copy

    def core_stage(mat):
        return go(ring(mat, 0, parts.at[mat, 1 - c], core_in.at[mat], core_peer))

    def wide(value):
        return value.astype(jnp.float32)

    half = parts.shape[3] // 2

    def half_stage(mat, core_copy):
        core_copy.wait_recv()
        sums[mat] = (wide(parts[mat, c]) + wide(core_in[mat])).astype(jnp.bfloat16)
        far = lax.rem(y + 2, 4)
        return (
            go(ring(mat, 1, sums.at[mat, far, pl.ds(0, half)], half_up_in.at[mat], y_up)),
            go(ring(mat, 2, sums.at[mat, far, pl.ds(half, half)], half_down_in.at[mat], y_down)),
        )

    def full_stage(mat, copies):
        above = lax.rem(y + 1, 4)
        below = lax.rem(y + 3, 4)
        copies[0].wait_recv()
        low = pl.ds(0, half)
        sums[mat, above, low] = (wide(sums[mat, above, low]) + wide(half_up_in[mat])).astype(
            jnp.bfloat16
        )
        first = go(ring(mat, 3, sums.at[mat, above], full_up_in.at[mat], y_up))
        copies[1].wait_recv()
        high = pl.ds(half, half)
        sums[mat, below, high] = (wide(sums[mat, below, high]) + wide(half_down_in[mat])).astype(
            jnp.bfloat16
        )
        return (first, go(ring(mat, 4, sums.at[mat, below], full_down_in.at[mat], y_down)))

    def finish(mat, copies, out_ref):
        for copy in copies:
            copy.wait_recv()
        out_ref[0] = (wide(sums[mat, y]) + wide(full_up_in[mat]) + wide(full_down_in[mat])).astype(
            jnp.bfloat16
        )

    def weight_copy(index, rows, dy, to):
        part = down_in.at[c, lax.rem(y + dy, 4), rows]
        return pltpu.make_async_remote_copy(
            src_ref=part,
            dst_ref=part,
            send_sem=weight_send.at[index],
            recv_sem=weight_recv.at[index],
            device_id=to,
            device_id_type=MESH,
        )

    owned = down_in.shape[2]
    every, low, high = pl.ds(0, owned), pl.ds(0, owned // 2), pl.ds(owned // 2, owned // 2)
    weight_own = [
        go(weight_copy(0, every, 0, y_up)),
        go(weight_copy(1, every, 0, y_down)),
        go(weight_copy(2, every, 0, core_peer)),
    ]
    weight_own[0].wait_recv()
    weight_above = go(weight_copy(3, low, 3, y_up))
    weight_core = [go(weight_copy(5, every, 3, core_peer))]
    weight_own[1].wait_recv()
    weight_below = go(weight_copy(4, high, 1, y_down))
    weight_core.append(go(weight_copy(6, every, 1, core_peer)))
    weight_above.wait_recv()
    weight_below.wait_recv()
    weight_core.append(go(weight_copy(7, every, 2, core_peer)))
    for copy in (weight_own[2], *weight_core):
        copy.wait_recv()
    gate, up = (weights_ref[n].reshape(-1, width) for n in range(2))
    down = down_in[...].reshape(-1, width)
    output_grads = flat(cot_in)
    hidden_grad = contract_cols(output_grads, down)
    arrive(rows_copies)
    expert_rows = flat(rows_in)
    gate_act = contract_cols(expert_rows, gate)
    up_act = contract_cols(expert_rows, up)
    hidden_units = swiglu_forward(gate_act, up_act)
    partial(0, hidden_units, output_grads)
    core_down = core_stage(0)
    gate_grad, up_grad = swiglu_backward(gate_act, up_act, hidden_grad)
    partial(1, gate_grad, expert_rows)
    core_gate = core_stage(1)
    half_down = half_stage(0, core_down)
    partial(2, up_grad, expert_rows)
    core_up = core_stage(2)
    half_gate = half_stage(1, core_gate)
    for start in range(0, width, chunk):
        out_buf[:, :, :, pl.ds(start, chunk)] = (
            jnp.dot(
                hidden_units,
                down[:, start : start + chunk],
                preferred_element_type=jnp.float32,
            )
            .astype(jnp.bfloat16)
            .reshape(2, experts, capacity, chunk)
        )
    own_out = pltpu.make_async_copy(out_buf.at[zl, ex], out_in.at[zl, ex], local_sem.at[2])
    own_out.start()
    back = []
    for index, (dz, de) in enumerate(offsets):
        if index:
            tz, te = peer(dz, de)
            copy = push(
                2, index, out_buf.at[tz, te], out_in.at[zl, ex], neighbour(zl=tz, exp=te)
            )
            copy.start()
            back.append(copy)
    full_down = full_stage(0, half_down)
    half_up = half_stage(2, core_up)
    full_gate = full_stage(1, half_gate)
    full_up = full_stage(2, half_up)
    finish(0, full_down, grad_down_ref)
    arrive((own_out, back))
    for start in range(0, width, chunk):
        cols = pl.ds(start, chunk)
        returned = out_in[:, :, :, cols].reshape(tokens, chunk)
        layer_ref[:, cols] = (
            wide(hidden_ref[:, cols])
            + jnp.dot(combine_ref[...], returned, preferred_element_type=jnp.float32)
        ).astype(jnp.bfloat16)
    finish(1, full_gate, grad_gate_ref)
    finish(2, full_up, grad_up_ref)
    for copy in (*rows_copies[1], *back, *started):
        copy.wait_send()


def expert_layer(send_rows, grad_rows, weights, w_down, hidden_state, dispatch_table):
    experts, capacity, width = send_rows.shape
    owned = weights.shape[3]
    token_count = hidden_state.shape[0]
    combine = jnp.concatenate([dispatch_table, dispatch_table], axis=0).T
    vmem = pl.BlockSpec(memory_space=pltpu.VMEM)
    bf16 = jnp.bfloat16
    landing = pltpu.VMEM((2, experts, capacity, width), bf16)
    grad_shape = jax.ShapeDtypeStruct((1, owned, width), bf16)
    return pl.pallas_call(
        expert_kernel,
        out_shape=(jax.ShapeDtypeStruct((token_count, width), bf16),) + (grad_shape,) * 3,
        in_specs=[vmem] * 6,
        out_specs=(vmem,) * 4,
        scratch_shapes=[
            landing,
            pltpu.VMEM((2, 4, owned, width), bf16),
            landing,
            landing,
            pltpu.VMEM((3, 2, 4, owned, width), bf16),
            pltpu.VMEM((3, 4, owned, width), bf16),
            pltpu.VMEM((3, 4, owned, width), bf16),
            pltpu.VMEM((3, owned // 2, width), bf16),
            pltpu.VMEM((3, owned // 2, width), bf16),
            pltpu.VMEM((3, owned, width), bf16),
            pltpu.VMEM((3, owned, width), bf16),
            pltpu.SemaphoreType.DMA((3, 2 * experts)),
            pltpu.SemaphoreType.DMA((3, 2 * experts)),
            pltpu.SemaphoreType.DMA((3, 5)),
            pltpu.SemaphoreType.DMA((3, 5)),
            pltpu.SemaphoreType.DMA((8,)),
            pltpu.SemaphoreType.DMA((8,)),
            pltpu.SemaphoreType.DMA((3,)),
        ],
        compiler_params=pltpu.CompilerParams(
            collective_id=1, has_side_effects=True, vmem_limit_bytes=56 * 2**20
        ),
        cost_estimate=pl.CostEstimate(
            flops=5_000_000_000, bytes_accessed=20_000_000, transcendentals=200_000
        ),
        name="experts",
    )(send_rows, grad_rows, weights, w_down, hidden_state, combine)


def local(
    resid,
    queries,
    keyvals,
    out_proj,
    norm_gain,
    token_ids,
    hash_table,
    w_gate,
    w_up,
    w_down,
    cotangent,
):
    token_count = resid.shape[0]
    model_width = resid.shape[1]
    expert_count = lax.axis_size("exp")
    capacity = token_count // expert_count
    expert_of = jnp.take(hash_table, token_ids)
    onehot_slots = (
        expert_of[:, None] == jnp.arange(expert_count, dtype=jnp.int32)[None, :]
    ).astype(jnp.int32)
    earlier = jnp.cumsum(onehot_slots, axis=0) - onehot_slots
    slot_of = jnp.sum(onehot_slots * earlier, axis=1)
    target = jnp.where(slot_of < capacity, expert_of * capacity + slot_of, -1)
    dispatch_table = (
        jnp.arange(expert_count * capacity, dtype=jnp.int32)[:, None] == target[None, :]
    ).astype(jnp.bfloat16)

    def placed(rows):
        return (
            jnp.dot(dispatch_table, rows, preferred_element_type=jnp.float32)
            .astype(jnp.bfloat16)
            .reshape(expert_count, capacity, model_width)
        )

    token_heads, grad_rows, weights = attend(
        queries, keyvals, placed(cotangent), w_gate, w_up
    )
    projected = contract_rows(token_heads.reshape(-1, token_count), out_proj)
    hidden_state = (resid.astype(jnp.float32) + projected).astype(jnp.bfloat16)
    widened = hidden_state.astype(jnp.float32)
    mean_square = jnp.mean(widened * widened, axis=1, keepdims=True)
    normed = (widened * lax.rsqrt(mean_square + norm_eps) * norm_gain.astype(jnp.float32)).astype(
        jnp.bfloat16
    )
    return expert_layer(
        placed(normed), grad_rows, weights, w_down, hidden_state, dispatch_table
    )


def solution(mesh):
    fine_mesh = Mesh(mesh.devices.reshape(2, 4, 2, 8), ("zl", "y", "c", "exp"))
    token_spec = P((*SEQ, "exp"), None)
    weight_spec = P("exp", SEQ, None)
    in_specs = (
        token_spec,
        P(SEQ, "exp"),
        P(SEQ, "exp"),
        P(),
        P(),
        P((*SEQ, "exp")),
        P(),
        weight_spec,
        weight_spec,
        weight_spec,
        token_spec,
    )
    out_specs = (token_spec, weight_spec, weight_spec, weight_spec)
    return jax.shard_map(
        local, mesh=fine_mesh, in_specs=in_specs, out_specs=out_specs, check_vma=False
    )
```

```python
import functools
import math

import jax
import jax.numpy as jnp
from jax import lax
from jax.experimental import pallas as pl
from jax.experimental.pallas import tpu as pltpu
from jax.sharding import Mesh
from jax.sharding import PartitionSpec as P

HEAD_DIM = 64
SEQ = ("zl", "y", "c")
MESH = pl.DeviceIdType.MESH
score_to_log2 = math.log2(math.e) / math.sqrt(HEAD_DIM)
very_negative = -1e30
norm_eps = 1e-05


def contract_rows(first_operand, second_operand):
    return lax.dot_general(
        first_operand, second_operand, (((0,), (0,)), ((), ())), preferred_element_type=jnp.float32
    )


def contract_cols(first_operand, second_operand):
    return lax.dot_general(
        first_operand, second_operand, (((1,), (1,)), ((), ())), preferred_element_type=jnp.float32
    )


def swiglu_forward(gate_act, up_act):
    sigmoid_gate = jax.nn.sigmoid(gate_act)
    silu_gate = gate_act * sigmoid_gate
    return (silu_gate * up_act).astype(jnp.bfloat16)


def swiglu_backward(gate_act, up_act, hidden_grad):
    sigmoid_gate = jax.nn.sigmoid(gate_act)
    silu_gate = gate_act * sigmoid_gate
    gate_grad = (
        hidden_grad * up_act * sigmoid_gate * (1.0 + gate_act * (1.0 - sigmoid_gate))
    ).astype(jnp.bfloat16)
    up_grad = (hidden_grad * silu_gate).astype(jnp.bfloat16)
    return (gate_grad, up_grad)


def neighbour(**place):
    return {axis: place.get(axis, lax.axis_index(axis)) for axis in (*SEQ, "exp")}


ARRIVALS = (
    (0, 0, 0),
    (0, 0, 1),
    (0, 3, 0),
    (0, 1, 0),
    (1, 0, 0),
    (0, 2, 0),
    (0, 3, 1),
    (0, 1, 1),
    (1, 0, 1),
    (1, 3, 0),
    (1, 1, 0),
    (1, 2, 0),
    (0, 2, 1),
    (1, 3, 1),
    (1, 1, 1),
    (1, 2, 1),
)
PASS_TURNS = {
    (0, 3, 0): 2,
    (0, 1, 0): 2,
    (1, 0, 0): 4,
    (0, 2, 0): 5,
    (1, 3, 0): 7,
    (1, 1, 0): 8,
    (1, 2, 0): 8,
}
KEY_PIECE = 256
ODD_LAG = 2
FAR_START = 2
WEIGHTS_START = 4
PUSH_START = 9
WEIGHTS_PASS = 17


def attention_kernel(
    queries_ref,
    keyvals_ref,
    grads_ref,
    gate_ref,
    up_ref,
    heads_out,
    grads_out,
    weights_out,
    kv_all,
    odd_out,
    odd_in,
    turned,
    m_ref,
    peak_ref,
    scores_ref,
    acc_ref,
    mixed_ref,
    kv_send,
    kv_recv,
    odd_sem,
    push_send,
    push_recv,
    heads_send,
    heads_recv,
    weight_send,
    weight_recv,
    local_sem,
):
    zl, y, c, ex = (lax.axis_index(a) for a in (*SEQ, "exp"))
    half_rows = odd_in.shape[1]
    heads = odd_in.shape[0] // HEAD_DIM
    pieces = half_rows // 128
    experts = grads_ref.shape[0]
    shard = zl * 8 + y * 2 + c
    mirror = 15 - shard
    core_peer = neighbour(c=1 - c)
    z_peer = neighbour(zl=1 - zl)
    y_up = neighbour(y=lax.rem(y + 1, 4))
    y_down = neighbour(y=lax.rem(y + 3, 4))
    y_far = neighbour(y=lax.rem(y + 2, 4))

    def mirrored(e):
        return {"zl": 1 - zl, "y": 3 - y, "c": 1 - c, "exp": e}

    barrier = pltpu.get_barrier_semaphore()
    greeted = [core_peer, y_up, y_down, y_far]
    for d in range(experts):
        e = lax.rem(ex + d, experts)
        greeted += [mirrored(e), neighbour(zl=1 - zl, exp=e)]
        if d:
            greeted.append(neighbour(exp=e))
    for other in greeted:
        pl.semaphore_signal(barrier, inc=1, device_id=other, device_id_type=MESH)

    own_weights = [
        pltpu.make_async_copy(ref.at[0], weights_out.at[n, c, y], local_sem.at[n])
        for n, ref in enumerate((gate_ref, up_ref))
    ]
    own_grads = pltpu.make_async_copy(grads_ref.at[ex], grads_out.at[zl, ex], local_sem.at[3])
    for copy in (*own_weights, own_grads):
        copy.start()

    keyvals = keyvals_ref[...]
    kv_all[shard, pl.ds(0, half_rows), :] = jnp.concatenate(
        [keyvals[:half_rows, :HEAD_DIM], keyvals[half_rows:, :HEAD_DIM]], axis=1
    )
    values = keyvals.T[HEAD_DIM:]
    for p in range(2 * pieces):
        kv_all[shard, pl.ds(half_rows + p * HEAD_DIM, HEAD_DIM), :] = values[
            :, p * 128 : (p + 1) * 128
        ]

    def turn(half, flipped):
        flat = jnp.concatenate(
            [flipped[h * HEAD_DIM : (h + 1) * HEAD_DIM] for h in range(heads)], axis=1
        )
        empty = jnp.zeros_like(flat)
        turned[half, 0] = jnp.concatenate([flat, empty], axis=0)
        turned[half, 1] = jnp.concatenate([empty, flat], axis=0)

    odd_out[...] = queries_ref[:, pl.ds(half_rows, half_rows)]
    turn(0, queries_ref[:, pl.ds(0, half_rows)])
    m_ref[...] = jnp.full_like(m_ref, very_negative)
    acc_ref[...] = jnp.zeros_like(acc_ref)
    pl.semaphore_wait(barrier, len(greeted))

    odd_copy = pltpu.make_async_remote_copy(
        src_ref=odd_out,
        dst_ref=odd_in,
        send_sem=odd_sem.at[0],
        recv_sem=odd_sem.at[1],
        device_id=mirrored(ex),
        device_id_type=MESH,
    )

    def shard_at(dz, dy, dc):
        return lax.rem(zl + dz, 2) * 8 + lax.rem(y + dy, 4) * 2 + lax.rem(c + dc, 2)

    def pass_on(index, t, to):
        return pltpu.make_async_remote_copy(
            src_ref=kv_all.at[t],
            dst_ref=kv_all.at[t],
            send_sem=kv_send.at[index],
            recv_sem=kv_recv.at[t],
            device_id=to,
            device_id_type=MESH,
        )

    routes = {
        (0, 0, 0): (z_peer, y_up, y_down, core_peer, y_far),
        (0, 3, 0): (z_peer, core_peer),
        (0, 1, 0): (z_peer, core_peer),
        (1, 0, 0): (y_far, core_peer),
        (0, 2, 0): (core_peer,),
        (1, 3, 0): (core_peer,),
        (1, 1, 0): (core_peer,),
        (1, 2, 0): (core_peer,),
    }
    forwards = {}
    for place, targets in routes.items():
        first = sum(len(f) for f in forwards.values())
        forwards[place] = [
            pass_on(first + n, shard_at(*place), to) for n, to in enumerate(targets)
        ]

    def weight_copy(index, rows, dy, to, dc=0):
        part = weights_out.at[:, lax.rem(c + dc, 2), lax.rem(y + dy, 4), rows]
        return pltpu.make_async_remote_copy(
            src_ref=part,
            dst_ref=part,
            send_sem=weight_send.at[index],
            recv_sem=weight_recv.at[index],
            device_id=to,
            device_id_type=MESH,
        )

    owned = weights_out.shape[3]
    every, low, high = pl.ds(0, owned), pl.ds(0, owned // 2), pl.ds(owned // 2, owned // 2)
    weight_own = [
        weight_copy(0, every, 0, y_up),
        weight_copy(1, every, 0, y_down),
        weight_copy(2, every, 0, core_peer),
    ]
    weight_above = weight_copy(3, low, 3, y_up)
    weight_below = weight_copy(4, high, 1, y_down)
    weight_core = [
        weight_copy(5, every, 3, core_peer),
        weight_copy(6, every, 1, core_peer),
        weight_copy(7, every, 2, core_peer),
    ]

    pushes = []
    for index in range(1, 2 * experts):
        dz, de = divmod(index, experts)
        e = lax.rem(ex + de, experts)
        pushes.append(
            pltpu.make_async_remote_copy(
                src_ref=grads_ref.at[e],
                dst_ref=grads_out.at[zl, ex],
                send_sem=push_send.at[index],
                recv_sem=push_recv.at[index],
                device_id=neighbour(zl=lax.rem(zl + dz, 2), exp=e),
                device_id_type=MESH,
            )
        )

    odd_copy.start()
    for copy in forwards[(0, 0, 0)][:4]:
        copy.start()

    ones = jnp.ones((16, half_rows), jnp.bfloat16)

    def values_of(block, part):
        turned_values = [
            kv_all[block, pl.ds(half_rows + (part * pieces + p) * HEAD_DIM, HEAD_DIM), :]
            for p in range(pieces)
        ]
        return jnp.concatenate([jnp.concatenate(turned_values, axis=1), ones], axis=0)

    def columns(head):
        return slice(head * half_rows, (head + 1) * half_rows)

    key_pieces = [pl.ds(start, KEY_PIECE) for start in range(0, half_rows, KEY_PIECE)]

    def score(half, block, part, rows, head, masked):
        s = (
            jnp.dot(
                kv_all[block, rows, :],
                turned[half, part, :, columns(head)],
                preferred_element_type=jnp.float32,
            )
            * score_to_log2
        )
        if masked:
            key_place = rows.start + lax.broadcasted_iota(jnp.int32, s.shape, 0)
            query_place = lax.broadcasted_iota(jnp.int32, s.shape, 1)
            s = jnp.where(key_place <= query_place, s, very_negative)
        return s

    def stage(slot, half, block, following=None):
        new = peak_ref[...]
        shrink = jnp.exp2(m_ref[half] - new)
        m_ref[half] = new
        if following is not None:
            next_half, next_block, masked = following
            start = m_ref[next_half]
        for head in range(heads):
            cols = columns(head)
            total = acc_ref[half, :, cols] * shrink[:, cols]
            if following is not None:
                peak = start[:, cols]
            for part in range(2):
                values = values_of(block, part)
                for rows in key_pieces:
                    if following is not None:
                        s = score(next_half, next_block, part, rows, head, masked and part == 1)
                        scores_ref[1 - slot, part, rows, cols] = s
                        peak = jnp.maximum(peak, jnp.max(s, axis=0, keepdims=True))
                    weights = jnp.exp2(scores_ref[slot, part, rows, cols] - new[:, cols])
                    total += jnp.dot(
                        values[:, rows.start : rows.start + KEY_PIECE],
                        weights.astype(jnp.bfloat16),
                        preferred_element_type=jnp.float32,
                    )
            acc_ref[half, :, cols] = total
            if following is not None:
                peak_ref[:, cols] = peak

    for head in range(heads):
        cols = columns(head)
        peak = m_ref[0, :, cols]
        for rows in key_pieces:
            s = score(0, shard, 0, rows, head, True)
            scores_ref[0, 0, rows, cols] = s
            scores_ref[0, 1, rows, cols] = jnp.full_like(s, very_negative)
            peak = jnp.maximum(peak, jnp.max(s, axis=0, keepdims=True))
        peak_ref[:, cols] = peak

    def slot_shard(slot):
        def pick(axis):
            return sum(
                jnp.where(slot == n, place[axis], 0) for n, place in enumerate(ARRIVALS)
            )

        return shard_at(pick(0), pick(1), pick(2))

    def visit(slot, carry):
        for n, place in enumerate(ARRIVALS):
            if place in PASS_TURNS:

                @pl.when(slot == PASS_TURNS[place])
                def _():
                    pass_on(0, shard_at(*place), core_peer).wait_recv()
                    for copy in forwards[place]:
                        copy.start()

            elif n:

                @pl.when(slot == n)
                def _():
                    pass_on(0, shard_at(*place), core_peer).wait_recv()

        @pl.when(slot == FAR_START)
        def _():
            forwards[(0, 0, 0)][4].start()

        @pl.when(slot == ODD_LAG)
        def _():
            odd_copy.wait_recv()
            turn(1, odd_in[...])

        @pl.when(slot == WEIGHTS_START)
        def _():
            for copy in own_weights:
                copy.wait()
            for copy in weight_own:
                copy.start()

        @pl.when(slot == PUSH_START)
        def _():
            for copy in pushes:
                copy.start()

        @pl.when(slot == WEIGHTS_PASS)
        def _():
            weight_own[0].wait_recv()
            weight_above.start()
            weight_core[0].start()
            weight_own[1].wait_recv()
            weight_below.start()
            weight_core[1].start()

        def one_half(half, inner):
            last_half, last_block, scored = inner
            seen = slot - ODD_LAG * half
            t = slot_shard(seen)
            here = (seen >= 0) & (seen < len(ARRIVALS))

            used = here & (t < jnp.where(half == 0, shard, mirror))
            for now in range(2):

                @pl.when(used & (scored == now))
                def _():
                    stage(now, last_half, last_block, (half, t, False))

            return (
                jnp.where(used, half, last_half),
                jnp.where(used, t, last_block),
                jnp.where(used, 1 - scored, scored),
            )

        return lax.fori_loop(0, 2, one_half, carry)

    last_half, last_block, _ = lax.fori_loop(
        0, len(ARRIVALS) + ODD_LAG, visit, (jnp.int32(0), shard, jnp.int32(0))
    )
    stage(1, last_half, last_block, (1, mirror, True))
    stage(0, 1, mirror)

    for half in range(2):
        total = acc_ref[half]
        mixed = total[:HEAD_DIM] / total[HEAD_DIM : HEAD_DIM + 1]
        for head in range(heads):
            for block in range(pieces):
                start = head * half_rows + block * 128
                mixed_ref[half, block, pl.ds(head * HEAD_DIM, HEAD_DIM), :] = mixed[
                    :, start : start + 128
                ].astype(jnp.bfloat16)

    def head_copy(half, block, to):
        return pltpu.make_async_remote_copy(
            src_ref=mixed_ref.at[half, block],
            dst_ref=heads_out.at[ex],
            send_sem=heads_send.at[half, block],
            recv_sem=heads_recv.at[ex],
            device_id=to,
            device_id_type=MESH,
        )

    even_copies = []
    for d in range(4):
        block = lax.rem(ex + d, 4)
        even_copies.append(head_copy(0, block, neighbour(exp=block)))
    odd_copies = []
    for d in range(4):
        block = lax.rem(ex + d, 4)
        odd_copies.append(head_copy(1, block, mirrored(4 + block)))
    own_heads = pltpu.make_async_copy(
        mixed_ref.at[0, lax.rem(ex, 4)], heads_out.at[ex], local_sem.at[4]
    )
    for copy in (*odd_copies, *even_copies[1:]):
        copy.start()

    @pl.when(ex < 4)
    def _():
        own_heads.start()

    @pl.when(ex >= 4)
    def _():
        even_copies[0].start()

    weight_above.wait_recv()
    weight_below.wait_recv()
    weight_core[2].start()

    def head_arrival(e):
        return pltpu.make_async_remote_copy(
            src_ref=mixed_ref.at[0, 0],
            dst_ref=heads_out.at[e],
            send_sem=heads_send.at[0, 0],
            recv_sem=heads_recv.at[e],
            device_id=core_peer,
            device_id_type=MESH,
        )

    for d in range(1, experts):
        head_arrival(lax.rem(ex + d, experts)).wait_recv()

    @pl.when(ex < 4)
    def _():
        own_heads.wait()

    @pl.when(ex >= 4)
    def _():
        head_arrival(ex).wait_recv()
        even_copies[0].wait_send()

    own_grads.wait()
    for copy in pushes:
        copy.wait()
    weight_own[2].wait_recv()
    for copy in weight_core:
        copy.wait_recv()
    odd_copy.wait_send()
    for copies in forwards.values():
        for copy in copies:
            copy.wait_send()
    for copy in (*weight_own, weight_above, weight_below, *weight_core):
        copy.wait_send()
    for copy in (*odd_copies, *even_copies[1:]):
        copy.wait_send()


def attend(queries, keyvals, send_grads, w_gate, w_up):
    query_width, row_count = queries.shape
    half_rows = row_count // 2
    heads = query_width // HEAD_DIM
    experts, capacity, width = send_grads.shape
    owned = w_gate.shape[1]
    bf16 = jnp.bfloat16
    vmem = pl.BlockSpec(memory_space=pltpu.VMEM)
    anywhere = pl.BlockSpec(memory_space=pl.ANY)
    dma = pltpu.SemaphoreType.DMA
    return pl.pallas_call(
        attention_kernel,
        out_shape=(
            jax.ShapeDtypeStruct((experts, query_width, row_count // experts), bf16),
            jax.ShapeDtypeStruct((2, experts, capacity, width), bf16),
            jax.ShapeDtypeStruct((2, 2, 4, owned, width), bf16),
        ),
        in_specs=[vmem] * 2 + [anywhere] * 3,
        out_specs=(anywhere,) * 3,
        scratch_shapes=[
            pltpu.VMEM((len(ARRIVALS), row_count, 2 * HEAD_DIM), bf16),
            pltpu.VMEM((query_width, half_rows), bf16),
            pltpu.VMEM((query_width, half_rows), bf16),
            pltpu.VMEM((2, 2, 2 * HEAD_DIM, heads * half_rows), bf16),
            pltpu.VMEM((2, 1, heads * half_rows), jnp.float32),
            pltpu.VMEM((1, heads * half_rows), jnp.float32),
            pltpu.VMEM((2, 2, half_rows, heads * half_rows), jnp.float32),
            pltpu.VMEM((2, HEAD_DIM + 16, heads * half_rows), jnp.float32),
            pltpu.VMEM((2, half_rows // 128, query_width, 128), bf16),
            dma((15,)),
            dma((len(ARRIVALS),)),
            dma((2,)),
            dma((2 * experts,)),
            dma((2 * experts,)),
            dma((2, 4)),
            dma((experts,)),
            dma((8,)),
            dma((8,)),
            dma((5,)),
        ],
        compiler_params=pltpu.CompilerParams(
            collective_id=0, has_side_effects=True, vmem_limit_bytes=48 * 2**20
        ),
        cost_estimate=pl.CostEstimate(
            flops=20_000_000_000, bytes_accessed=20_000_000, transcendentals=27_000_000
        ),
        name="attention",
    )(queries, keyvals, send_grads, w_gate, w_up)


def expert_kernel(
    rows_ref,
    cot_ref,
    weights_ref,
    own_down_ref,
    hidden_ref,
    dispatch_ref,
    layer_ref,
    grad_gate_ref,
    grad_up_ref,
    grad_down_ref,
    rows_in,
    cot_in,
    weights_in,
    down_in,
    out_buf,
    out_in,
    parts,
    core_in,
    sums,
    half_up_in,
    half_down_in,
    full_up_in,
    full_down_in,
    push_send,
    push_recv,
    ring_send,
    ring_recv,
    weight_send,
    weight_recv,
    local_sem,
):
    zl, y, c, ex = (lax.axis_index(a) for a in (*SEQ, "exp"))
    experts = rows_ref.shape[0]
    capacity, width = rows_ref.shape[1:]
    tokens = 2 * experts * capacity
    core_peer = neighbour(c=1 - c)
    y_up = neighbour(y=lax.rem(y + 1, 4))
    y_down = neighbour(y=lax.rem(y + 3, 4))
    offsets = [(dz, de) for dz in range(2) for de in range(experts)]

    def peer(dz, de):
        return lax.rem(zl + dz, 2), lax.rem(ex + de, experts)

    def source(dz, de):
        return lax.rem(zl + 2 - dz, 2), lax.rem(ex + experts - de, experts)

    own_down = pltpu.make_async_copy(own_down_ref.at[0], down_in.at[c, y], local_sem.at[0])
    load_weights = pltpu.make_async_copy(weights_ref, weights_in, local_sem.at[3])
    load_cot = pltpu.make_async_copy(cot_ref, cot_in, local_sem.at[4])
    own_down.start()
    barrier = pltpu.get_barrier_semaphore()
    for dz, de in offsets[1:]:
        tz, te = peer(dz, de)
        pl.semaphore_signal(
            barrier, inc=1, device_id=neighbour(zl=tz, exp=te), device_id_type=MESH
        )
    for other in (core_peer, y_up, y_down):
        pl.semaphore_signal(barrier, inc=1, device_id=other, device_id_type=MESH)
    pl.semaphore_wait(barrier, len(offsets) + 2)

    def push(kind, index, src, dst, to):
        return pltpu.make_async_remote_copy(
            src_ref=src,
            dst_ref=dst,
            send_sem=push_send.at[kind, index],
            recv_sem=push_recv.at[kind, index],
            device_id=to,
            device_id_type=MESH,
        )

    def spread(kind, src_ref, dst_ref):
        own = pltpu.make_async_copy(src_ref.at[ex], dst_ref.at[zl, ex], local_sem.at[kind])
        own.start()
        sent = []
        for index, (dz, de) in enumerate(offsets):
            if index:
                tz, te = peer(dz, de)
                copy = push(
                    kind, index, src_ref.at[te], dst_ref.at[zl, ex], neighbour(zl=tz, exp=te)
                )
                copy.start()
                sent.append(copy)
        return own, sent

    def arrive(spread_copies):
        own, sent = spread_copies
        own.wait()
        for copy in sent:
            copy.wait_recv()

    rows_copies = spread(1, rows_ref, rows_in)

    def flat(ref):
        return ref[...].reshape(tokens, width)

    def ring(mat, stage, src, dst, to):
        return pltpu.make_async_remote_copy(
            src_ref=src,
            dst_ref=dst,
            send_sem=ring_send.at[mat, stage],
            recv_sem=ring_recv.at[mat, stage],
            device_id=to,
            device_id_type=MESH,
        )

    chunk = 512

    def partial(mat, first, second):
        turned = first.T
        for start in range(0, width, chunk):
            part = jnp.dot(
                turned, second[:, start : start + chunk], preferred_element_type=jnp.float32
            ).astype(jnp.bfloat16)
            parts[mat, :, :, :, pl.ds(start, chunk)] = part.reshape(2, 4, -1, chunk)

    started = []

    def go(copy):
        copy.start()
        started.append(copy)
        return copy

    def core_stage(mat):
        return go(ring(mat, 0, parts.at[mat, 1 - c], core_in.at[mat], core_peer))

    def wide(value):
        return value.astype(jnp.float32)

    half = parts.shape[3] // 2

    def half_stage(mat, core_copy):
        core_copy.wait_recv()
        sums[mat] = (wide(parts[mat, c]) + wide(core_in[mat])).astype(jnp.bfloat16)
        far = lax.rem(y + 2, 4)
        return (
            go(ring(mat, 1, sums.at[mat, far, pl.ds(0, half)], half_up_in.at[mat], y_up)),
            go(ring(mat, 2, sums.at[mat, far, pl.ds(half, half)], half_down_in.at[mat], y_down)),
        )

    def full_stage(mat, copies):
        above = lax.rem(y + 1, 4)
        below = lax.rem(y + 3, 4)
        copies[0].wait_recv()
        low = pl.ds(0, half)
        sums[mat, above, low] = (wide(sums[mat, above, low]) + wide(half_up_in[mat])).astype(
            jnp.bfloat16
        )
        first = go(ring(mat, 3, sums.at[mat, above], full_up_in.at[mat], y_up))
        copies[1].wait_recv()
        high = pl.ds(half, half)
        sums[mat, below, high] = (wide(sums[mat, below, high]) + wide(half_down_in[mat])).astype(
            jnp.bfloat16
        )
        return (first, go(ring(mat, 4, sums.at[mat, below], full_down_in.at[mat], y_down)))

    def finish(mat, copies, out_ref):
        for copy in copies:
            copy.wait_recv()
        out_ref[0] = (wide(sums[mat, y]) + wide(full_up_in[mat]) + wide(full_down_in[mat])).astype(
            jnp.bfloat16
        )

    def weight_copy(index, rows, dy, to):
        part = down_in.at[c, lax.rem(y + dy, 4), rows]
        return pltpu.make_async_remote_copy(
            src_ref=part,
            dst_ref=part,
            send_sem=weight_send.at[index],
            recv_sem=weight_recv.at[index],
            device_id=to,
            device_id_type=MESH,
        )

    own_down.wait()
    owned = down_in.shape[2]
    every, low, high = pl.ds(0, owned), pl.ds(0, owned // 2), pl.ds(owned // 2, owned // 2)
    weight_own = [
        go(weight_copy(0, every, 0, y_up)),
        go(weight_copy(1, every, 0, y_down)),
        go(weight_copy(2, every, 0, core_peer)),
    ]
    load_weights.start()
    load_cot.start()
    weight_own[0].wait_recv()
    weight_above = go(weight_copy(3, low, 3, y_up))
    weight_core = [go(weight_copy(5, every, 3, core_peer))]
    weight_own[1].wait_recv()
    weight_below = go(weight_copy(4, high, 1, y_down))
    weight_core.append(go(weight_copy(6, every, 1, core_peer)))
    weight_above.wait_recv()
    weight_below.wait_recv()
    weight_core.append(go(weight_copy(7, every, 2, core_peer)))
    for copy in (weight_own[2], *weight_core):
        copy.wait_recv()
    load_cot.wait()
    load_weights.wait()
    gate, up = (weights_in[n].reshape(-1, width) for n in range(2))
    down = down_in[...].reshape(-1, width)
    output_grads = flat(cot_in)
    hidden_grad = contract_cols(output_grads, down)
    arrive(rows_copies)
    expert_rows = flat(rows_in)
    gate_act = contract_cols(expert_rows, gate)
    up_act = contract_cols(expert_rows, up)
    hidden_units = swiglu_forward(gate_act, up_act)
    partial(0, hidden_units, output_grads)
    core_down = core_stage(0)
    gate_grad, up_grad = swiglu_backward(gate_act, up_act, hidden_grad)
    partial(1, gate_grad, expert_rows)
    core_gate = core_stage(1)
    half_down = half_stage(0, core_down)
    partial(2, up_grad, expert_rows)
    core_up = core_stage(2)
    half_gate = half_stage(1, core_gate)
    for start in range(0, width, chunk):
        out_buf[:, :, :, pl.ds(start, chunk)] = (
            jnp.dot(
                hidden_units,
                down[:, start : start + chunk],
                preferred_element_type=jnp.float32,
            )
            .astype(jnp.bfloat16)
            .reshape(2, experts, capacity, chunk)
        )
    own_out = pltpu.make_async_copy(out_buf.at[zl, ex], out_in.at[zl, ex], local_sem.at[2])
    own_out.start()
    back = []
    for index, (dz, de) in enumerate(offsets):
        if index:
            tz, te = peer(dz, de)
            copy = push(
                2, index, out_buf.at[tz, te], out_in.at[zl, ex], neighbour(zl=tz, exp=te)
            )
            copy.start()
            back.append(copy)
    full_down = full_stage(0, half_down)
    half_up = half_stage(2, core_up)
    full_gate = full_stage(1, half_gate)
    full_up = full_stage(2, half_up)
    finish(0, full_down, grad_down_ref)
    arrive((own_out, back))
    for start in range(0, width, chunk):
        cols = pl.ds(start, chunk)
        combined = sum(
            contract_rows(dispatch_ref[...], out_in[z, :, :, cols].reshape(-1, chunk))
            for z in range(2)
        )
        layer_ref[:, cols] = (wide(hidden_ref[:, cols]) + combined).astype(jnp.bfloat16)
    finish(1, full_gate, grad_gate_ref)
    finish(2, full_up, grad_up_ref)
    for copy in (*rows_copies[1], *back, *started):
        copy.wait_send()


def hand_on_kernel(*refs):
    for source, result in zip(refs[:4], refs[4:]):
        result[...] = source[...]


def expert_layer(send_rows, grad_rows, weights, w_down, hidden_state, dispatch_table):
    experts, capacity, width = send_rows.shape
    owned = weights.shape[3]
    token_count = hidden_state.shape[0]
    vmem = pl.BlockSpec(memory_space=pltpu.VMEM)
    anywhere = pl.BlockSpec(memory_space=pl.ANY)
    bf16 = jnp.bfloat16
    landing = pltpu.VMEM((2, experts, capacity, width), bf16)
    grad_shape = jax.ShapeDtypeStruct((1, owned, width), bf16)
    results = pl.pallas_call(
        expert_kernel,
        out_shape=(jax.ShapeDtypeStruct((token_count, width), bf16),) + (grad_shape,) * 3,
        in_specs=[anywhere] * 4 + [vmem] * 2,
        out_specs=(vmem,) * 4,
        scratch_shapes=[
            landing,
            landing,
            pltpu.VMEM(weights.shape, bf16),
            pltpu.VMEM((2, 4, owned, width), bf16),
            landing,
            landing,
            pltpu.VMEM((3, 2, 4, owned, width), bf16),
            pltpu.VMEM((3, 4, owned, width), bf16),
            pltpu.VMEM((3, 4, owned, width), bf16),
            pltpu.VMEM((3, owned // 2, width), bf16),
            pltpu.VMEM((3, owned // 2, width), bf16),
            pltpu.VMEM((3, owned, width), bf16),
            pltpu.VMEM((3, owned, width), bf16),
            pltpu.SemaphoreType.DMA((3, 2 * experts)),
            pltpu.SemaphoreType.DMA((3, 2 * experts)),
            pltpu.SemaphoreType.DMA((3, 5)),
            pltpu.SemaphoreType.DMA((3, 5)),
            pltpu.SemaphoreType.DMA((8,)),
            pltpu.SemaphoreType.DMA((8,)),
            pltpu.SemaphoreType.DMA((5,)),
        ],
        compiler_params=pltpu.CompilerParams(
            collective_id=1, has_side_effects=True, vmem_limit_bytes=56 * 2**20
        ),
        cost_estimate=pl.CostEstimate(
            flops=5_000_000_000, bytes_accessed=20_000_000, transcendentals=200_000
        ),
        name="experts",
    )(send_rows, grad_rows, weights, w_down, hidden_state, dispatch_table)
    return pl.pallas_call(
        hand_on_kernel,
        out_shape=[jax.ShapeDtypeStruct(r.shape, r.dtype) for r in results],
        in_specs=[vmem] * 4,
        out_specs=[vmem] * 4,
        name="hand_on",
    )(*results)


def local(
    resid,
    queries,
    keyvals,
    out_proj,
    norm_gain,
    token_ids,
    hash_table,
    w_gate,
    w_up,
    w_down,
    cotangent,
):
    token_count = resid.shape[0]
    model_width = resid.shape[1]
    expert_count = lax.axis_size("exp")
    capacity = token_count // expert_count
    expert_of = hash_table.at[token_ids].get(mode="promise_in_bounds")
    onehot_slots = (
        expert_of[:, None] == jnp.arange(expert_count, dtype=jnp.int32)[None, :]
    ).astype(jnp.int32)
    earlier = jnp.cumsum(onehot_slots, axis=0) - onehot_slots
    slot_of = jnp.sum(onehot_slots * earlier, axis=1)
    target = jnp.where(slot_of < capacity, expert_of * capacity + slot_of, -1)
    dispatch_table = (
        jnp.arange(expert_count * capacity, dtype=jnp.int32)[:, None] == target[None, :]
    ).astype(jnp.bfloat16)

    def placed(rows):
        return (
            jnp.dot(dispatch_table, rows, preferred_element_type=jnp.float32)
            .astype(jnp.bfloat16)
            .reshape(expert_count, capacity, model_width)
        )

    token_heads, grad_rows, weights = attend(
        queries.T, keyvals, placed(cotangent), w_gate, w_up
    )
    projected = contract_rows(token_heads.reshape(-1, token_count), out_proj)
    hidden_state = (resid.astype(jnp.float32) + projected).astype(jnp.bfloat16)
    widened = hidden_state.astype(jnp.float32)
    mean_square = jnp.mean(widened * widened, axis=1, keepdims=True)
    normed = (widened * lax.rsqrt(mean_square + norm_eps) * norm_gain.astype(jnp.float32)).astype(
        jnp.bfloat16
    )
    return expert_layer(
        placed(normed), grad_rows, weights, w_down, hidden_state, dispatch_table
    )


def solution(mesh):
    fine_mesh = Mesh(mesh.devices.reshape(2, 4, 2, 8), ("zl", "y", "c", "exp"))
    token_spec = P((*SEQ, "exp"), None)
    weight_spec = P("exp", SEQ, None)
    in_specs = (
        token_spec,
        P(SEQ, "exp"),
        P(SEQ, "exp"),
        P(),
        P(),
        P((*SEQ, "exp")),
        P(),
        weight_spec,
        weight_spec,
        weight_spec,
        token_spec,
    )
    out_specs = (token_spec, weight_spec, weight_spec, weight_spec)
    return jax.shard_map(
        local, mesh=fine_mesh, in_specs=in_specs, out_specs=out_specs, check_vma=False
    )
```

```python
import functools
import math

import jax
import jax.numpy as jnp
from jax import lax
from jax.experimental import pallas as pl
from jax.experimental.pallas import tpu as pltpu
from jax.sharding import Mesh
from jax.sharding import PartitionSpec as P

HEAD_DIM = 64
SEQ = ("zl", "y", "c")
MESH = pl.DeviceIdType.MESH
score_to_log2 = math.log2(math.e) / math.sqrt(HEAD_DIM)
very_negative = -1e30
norm_eps = 1e-05


def contract_rows(first_operand, second_operand):
    return lax.dot_general(
        first_operand, second_operand, (((0,), (0,)), ((), ())), preferred_element_type=jnp.float32
    )


def contract_cols(first_operand, second_operand):
    return lax.dot_general(
        first_operand, second_operand, (((1,), (1,)), ((), ())), preferred_element_type=jnp.float32
    )


def swiglu_forward(gate_act, up_act):
    sigmoid_gate = jax.nn.sigmoid(gate_act)
    silu_gate = gate_act * sigmoid_gate
    return (silu_gate * up_act).astype(jnp.bfloat16)


def swiglu_backward(gate_act, up_act, hidden_grad):
    sigmoid_gate = jax.nn.sigmoid(gate_act)
    silu_gate = gate_act * sigmoid_gate
    gate_grad = (
        hidden_grad * up_act * sigmoid_gate * (1.0 + gate_act * (1.0 - sigmoid_gate))
    ).astype(jnp.bfloat16)
    up_grad = (hidden_grad * silu_gate).astype(jnp.bfloat16)
    return (gate_grad, up_grad)


def neighbour(**place):
    return {axis: place.get(axis, lax.axis_index(axis)) for axis in (*SEQ, "exp")}


ARRIVALS = (
    (0, 0, 0),
    (0, 0, 1),
    (0, 3, 0),
    (0, 1, 0),
    (1, 0, 0),
    (0, 2, 0),
    (0, 3, 1),
    (0, 1, 1),
    (1, 0, 1),
    (1, 3, 0),
    (1, 1, 0),
    (1, 2, 0),
    (0, 2, 1),
    (1, 3, 1),
    (1, 1, 1),
    (1, 2, 1),
)
PASS_TURNS = {
    (0, 3, 0): 2,
    (0, 1, 0): 2,
    (1, 0, 0): 4,
    (0, 2, 0): 5,
    (1, 3, 0): 7,
    (1, 1, 0): 8,
    (1, 2, 0): 8,
}
KEY_PIECE = 256
ODD_LAG = 2
FAR_START = 2
WEIGHTS_START = 4
PUSH_START = 9
WEIGHTS_PASS = 17


def attention_kernel(
    queries_ref,
    keyvals_ref,
    grads_ref,
    gate_ref,
    up_ref,
    heads_out,
    grads_out,
    weights_out,
    kv_all,
    odd_out,
    odd_in,
    turned,
    m_ref,
    peak_ref,
    scores_ref,
    acc_ref,
    mixed_ref,
    kv_send,
    kv_recv,
    odd_sem,
    push_send,
    push_recv,
    heads_send,
    heads_recv,
    weight_send,
    weight_recv,
    local_sem,
):
    zl, y, c, ex = (lax.axis_index(a) for a in (*SEQ, "exp"))
    half_rows = odd_in.shape[1]
    heads = odd_in.shape[0] // HEAD_DIM
    pieces = half_rows // 128
    experts = grads_ref.shape[0]
    shard = zl * 8 + y * 2 + c
    mirror = 15 - shard
    core_peer = neighbour(c=1 - c)
    z_peer = neighbour(zl=1 - zl)
    y_up = neighbour(y=lax.rem(y + 1, 4))
    y_down = neighbour(y=lax.rem(y + 3, 4))
    y_far = neighbour(y=lax.rem(y + 2, 4))

    def mirrored(e):
        return {"zl": 1 - zl, "y": 3 - y, "c": 1 - c, "exp": e}

    barrier = pltpu.get_barrier_semaphore()
    greeted = [core_peer, y_up, y_down, y_far]
    for d in range(experts):
        e = lax.rem(ex + d, experts)
        greeted += [mirrored(e), neighbour(zl=1 - zl, exp=e)]
        if d:
            greeted.append(neighbour(exp=e))
    for other in greeted:
        pl.semaphore_signal(barrier, inc=1, device_id=other, device_id_type=MESH)

    own_weights = [
        pltpu.make_async_copy(ref.at[0], weights_out.at[n, c, y], local_sem.at[n])
        for n, ref in enumerate((gate_ref, up_ref))
    ]
    own_grads = pltpu.make_async_copy(grads_ref.at[ex], grads_out.at[zl, ex], local_sem.at[3])
    for copy in (*own_weights, own_grads):
        copy.start()

    keyvals = keyvals_ref[...]
    kv_all[shard, pl.ds(0, half_rows), :] = jnp.concatenate(
        [keyvals[:half_rows, :HEAD_DIM], keyvals[half_rows:, :HEAD_DIM]], axis=1
    )
    values = keyvals.T[HEAD_DIM:]
    for p in range(2 * pieces):
        kv_all[shard, pl.ds(half_rows + p * HEAD_DIM, HEAD_DIM), :] = values[
            :, p * 128 : (p + 1) * 128
        ]

    def turn(half, flipped):
        flat = jnp.concatenate(
            [flipped[h * HEAD_DIM : (h + 1) * HEAD_DIM] for h in range(heads)], axis=1
        )
        empty = jnp.zeros_like(flat)
        turned[half, 0] = jnp.concatenate([flat, empty], axis=0)
        turned[half, 1] = jnp.concatenate([empty, flat], axis=0)

    odd_out[...] = queries_ref[:, pl.ds(half_rows, half_rows)]
    turn(0, queries_ref[:, pl.ds(0, half_rows)])
    m_ref[...] = jnp.full_like(m_ref, very_negative)
    acc_ref[...] = jnp.zeros_like(acc_ref)
    pl.semaphore_wait(barrier, len(greeted))

    odd_copy = pltpu.make_async_remote_copy(
        src_ref=odd_out,
        dst_ref=odd_in,
        send_sem=odd_sem.at[0],
        recv_sem=odd_sem.at[1],
        device_id=mirrored(ex),
        device_id_type=MESH,
    )

    def shard_at(dz, dy, dc):
        return lax.rem(zl + dz, 2) * 8 + lax.rem(y + dy, 4) * 2 + lax.rem(c + dc, 2)

    def pass_on(index, t, to):
        return pltpu.make_async_remote_copy(
            src_ref=kv_all.at[t],
            dst_ref=kv_all.at[t],
            send_sem=kv_send.at[index],
            recv_sem=kv_recv.at[t],
            device_id=to,
            device_id_type=MESH,
        )

    routes = {
        (0, 0, 0): (z_peer, y_up, y_down, core_peer, y_far),
        (0, 3, 0): (z_peer, core_peer),
        (0, 1, 0): (z_peer, core_peer),
        (1, 0, 0): (y_far, core_peer),
        (0, 2, 0): (core_peer,),
        (1, 3, 0): (core_peer,),
        (1, 1, 0): (core_peer,),
        (1, 2, 0): (core_peer,),
    }
    forwards = {}
    for place, targets in routes.items():
        first = sum(len(f) for f in forwards.values())
        forwards[place] = [
            pass_on(first + n, shard_at(*place), to) for n, to in enumerate(targets)
        ]

    def weight_copy(index, rows, dy, to, dc=0):
        part = weights_out.at[:, lax.rem(c + dc, 2), lax.rem(y + dy, 4), rows]
        return pltpu.make_async_remote_copy(
            src_ref=part,
            dst_ref=part,
            send_sem=weight_send.at[index],
            recv_sem=weight_recv.at[index],
            device_id=to,
            device_id_type=MESH,
        )

    owned = weights_out.shape[3]
    every, low, high = pl.ds(0, owned), pl.ds(0, owned // 2), pl.ds(owned // 2, owned // 2)
    weight_own = [
        weight_copy(0, every, 0, y_up),
        weight_copy(1, every, 0, y_down),
        weight_copy(2, every, 0, core_peer),
    ]
    weight_above = weight_copy(3, low, 3, y_up)
    weight_below = weight_copy(4, high, 1, y_down)
    weight_core = [
        weight_copy(5, every, 3, core_peer),
        weight_copy(6, every, 1, core_peer),
        weight_copy(7, every, 2, core_peer),
    ]

    pushes = []
    for index in range(1, 2 * experts):
        dz, de = divmod(index, experts)
        e = lax.rem(ex + de, experts)
        pushes.append(
            pltpu.make_async_remote_copy(
                src_ref=grads_ref.at[e],
                dst_ref=grads_out.at[zl, ex],
                send_sem=push_send.at[index],
                recv_sem=push_recv.at[index],
                device_id=neighbour(zl=lax.rem(zl + dz, 2), exp=e),
                device_id_type=MESH,
            )
        )

    odd_copy.start()
    for copy in forwards[(0, 0, 0)][:4]:
        copy.start()

    ones = jnp.ones((16, half_rows), jnp.bfloat16)

    def values_of(block, part):
        turned_values = [
            kv_all[block, pl.ds(half_rows + (part * pieces + p) * HEAD_DIM, HEAD_DIM), :]
            for p in range(pieces)
        ]
        return jnp.concatenate([jnp.concatenate(turned_values, axis=1), ones], axis=0)

    def columns(head):
        return slice(head * half_rows, (head + 1) * half_rows)

    key_pieces = [pl.ds(start, KEY_PIECE) for start in range(0, half_rows, KEY_PIECE)]

    def score(half, block, part, rows, head, masked):
        s = (
            jnp.dot(
                kv_all[block, rows, :],
                turned[half, part, :, columns(head)],
                preferred_element_type=jnp.float32,
            )
            * score_to_log2
        )
        if masked:
            key_place = rows.start + lax.broadcasted_iota(jnp.int32, s.shape, 0)
            query_place = lax.broadcasted_iota(jnp.int32, s.shape, 1)
            s = jnp.where(key_place <= query_place, s, very_negative)
        return s

    def stage(slot, half, block, following=None):
        new = peak_ref[...]
        shrink = jnp.exp2(m_ref[half] - new)
        m_ref[half] = new
        if following is not None:
            next_half, next_block, masked = following
            start = m_ref[next_half]
        for head in range(heads):
            cols = columns(head)
            total = acc_ref[half, :, cols] * shrink[:, cols]
            if following is not None:
                peak = start[:, cols]
            for part in range(2):
                values = values_of(block, part)
                for rows in key_pieces:
                    if following is not None:
                        s = score(next_half, next_block, part, rows, head, masked and part == 1)
                        scores_ref[1 - slot, part, rows, cols] = s
                        peak = jnp.maximum(peak, jnp.max(s, axis=0, keepdims=True))
                    weights = jnp.exp2(scores_ref[slot, part, rows, cols] - new[:, cols])
                    total += jnp.dot(
                        values[:, rows.start : rows.start + KEY_PIECE],
                        weights.astype(jnp.bfloat16),
                        preferred_element_type=jnp.float32,
                    )
            acc_ref[half, :, cols] = total
            if following is not None:
                peak_ref[:, cols] = peak

    for head in range(heads):
        cols = columns(head)
        peak = m_ref[0, :, cols]
        for rows in key_pieces:
            s = score(0, shard, 0, rows, head, True)
            scores_ref[0, 0, rows, cols] = s
            scores_ref[0, 1, rows, cols] = jnp.full_like(s, very_negative)
            peak = jnp.maximum(peak, jnp.max(s, axis=0, keepdims=True))
        peak_ref[:, cols] = peak

    def slot_shard(slot):
        def pick(axis):
            return sum(
                jnp.where(slot == n, place[axis], 0) for n, place in enumerate(ARRIVALS)
            )

        return shard_at(pick(0), pick(1), pick(2))

    def visit(slot, carry):
        for n, place in enumerate(ARRIVALS):
            if place in PASS_TURNS:

                @pl.when(slot == PASS_TURNS[place])
                def _():
                    pass_on(0, shard_at(*place), core_peer).wait_recv()
                    for copy in forwards[place]:
                        copy.start()

            elif n:

                @pl.when(slot == n)
                def _():
                    pass_on(0, shard_at(*place), core_peer).wait_recv()

        @pl.when(slot == FAR_START)
        def _():
            forwards[(0, 0, 0)][4].start()

        @pl.when(slot == ODD_LAG)
        def _():
            odd_copy.wait_recv()
            turn(1, odd_in[...])

        @pl.when(slot == WEIGHTS_START)
        def _():
            for copy in own_weights:
                copy.wait()
            for copy in weight_own:
                copy.start()

        @pl.when(slot == PUSH_START)
        def _():
            for copy in pushes:
                copy.start()

        @pl.when(slot == WEIGHTS_PASS)
        def _():
            weight_own[0].wait_recv()
            weight_above.start()
            weight_core[0].start()
            weight_own[1].wait_recv()
            weight_below.start()
            weight_core[1].start()

        def one_half(half, inner):
            last_half, last_block, scored = inner
            seen = slot - ODD_LAG * half
            t = slot_shard(seen)
            here = (seen >= 0) & (seen < len(ARRIVALS))

            used = here & (t < jnp.where(half == 0, shard, mirror))
            for now in range(2):

                @pl.when(used & (scored == now))
                def _():
                    stage(now, last_half, last_block, (half, t, False))

            return (
                jnp.where(used, half, last_half),
                jnp.where(used, t, last_block),
                jnp.where(used, 1 - scored, scored),
            )

        return lax.fori_loop(0, 2, one_half, carry)

    last_half, last_block, _ = lax.fori_loop(
        0, len(ARRIVALS) + ODD_LAG, visit, (jnp.int32(0), shard, jnp.int32(0))
    )
    stage(1, last_half, last_block, (1, mirror, True))

    def settle(half):
        total = acc_ref[half]
        mixed = total[:HEAD_DIM] / total[HEAD_DIM : HEAD_DIM + 1]
        for head in range(heads):
            for block in range(pieces):
                start = head * half_rows + block * 128
                mixed_ref[half, block, pl.ds(head * HEAD_DIM, HEAD_DIM), :] = mixed[
                    :, start : start + 128
                ].astype(jnp.bfloat16)

    def head_copy(half, block, to):
        return pltpu.make_async_remote_copy(
            src_ref=mixed_ref.at[half, block],
            dst_ref=heads_out.at[ex],
            send_sem=heads_send.at[half, block],
            recv_sem=heads_recv.at[ex],
            device_id=to,
            device_id_type=MESH,
        )

    even_copies = []
    for d in range(4):
        block = lax.rem(ex + d, 4)
        even_copies.append(head_copy(0, block, neighbour(exp=block)))
    odd_copies = []
    for d in range(4):
        block = lax.rem(ex + d, 4)
        odd_copies.append(head_copy(1, block, mirrored(4 + block)))
    own_heads = pltpu.make_async_copy(
        mixed_ref.at[0, lax.rem(ex, 4)], heads_out.at[ex], local_sem.at[4]
    )
    settle(0)
    for copy in even_copies[1:]:
        copy.start()

    @pl.when(ex < 4)
    def _():
        own_heads.start()

    @pl.when(ex >= 4)
    def _():
        even_copies[0].start()

    stage(0, 1, mirror)
    settle(1)
    for copy in odd_copies:
        copy.start()

    weight_above.wait_recv()
    weight_below.wait_recv()
    weight_core[2].start()

    def head_arrival(e):
        return pltpu.make_async_remote_copy(
            src_ref=mixed_ref.at[0, 0],
            dst_ref=heads_out.at[e],
            send_sem=heads_send.at[0, 0],
            recv_sem=heads_recv.at[e],
            device_id=core_peer,
            device_id_type=MESH,
        )

    for d in range(1, experts):
        head_arrival(lax.rem(ex + d, experts)).wait_recv()

    @pl.when(ex < 4)
    def _():
        own_heads.wait()

    @pl.when(ex >= 4)
    def _():
        head_arrival(ex).wait_recv()
        even_copies[0].wait_send()

    own_grads.wait()
    for copy in pushes:
        copy.wait()
    weight_own[2].wait_recv()
    for copy in weight_core:
        copy.wait_recv()
    odd_copy.wait_send()
    for copies in forwards.values():
        for copy in copies:
            copy.wait_send()
    for copy in (*weight_own, weight_above, weight_below, *weight_core):
        copy.wait_send()
    for copy in (*odd_copies, *even_copies[1:]):
        copy.wait_send()


def attend(queries, keyvals, send_grads, w_gate, w_up):
    query_width, row_count = queries.shape
    half_rows = row_count // 2
    heads = query_width // HEAD_DIM
    experts, capacity, width = send_grads.shape
    owned = w_gate.shape[1]
    bf16 = jnp.bfloat16
    vmem = pl.BlockSpec(memory_space=pltpu.VMEM)
    anywhere = pl.BlockSpec(memory_space=pl.ANY)
    dma = pltpu.SemaphoreType.DMA
    return pl.pallas_call(
        attention_kernel,
        out_shape=(
            jax.ShapeDtypeStruct((experts, query_width, row_count // experts), bf16),
            jax.ShapeDtypeStruct((2, experts, capacity, width), bf16),
            jax.ShapeDtypeStruct((2, 2, 4, owned, width), bf16),
        ),
        in_specs=[vmem] * 2 + [anywhere] * 3,
        out_specs=(anywhere,) * 3,
        scratch_shapes=[
            pltpu.VMEM((len(ARRIVALS), row_count, 2 * HEAD_DIM), bf16),
            pltpu.VMEM((query_width, half_rows), bf16),
            pltpu.VMEM((query_width, half_rows), bf16),
            pltpu.VMEM((2, 2, 2 * HEAD_DIM, heads * half_rows), bf16),
            pltpu.VMEM((2, 1, heads * half_rows), jnp.float32),
            pltpu.VMEM((1, heads * half_rows), jnp.float32),
            pltpu.VMEM((2, 2, half_rows, heads * half_rows), jnp.float32),
            pltpu.VMEM((2, HEAD_DIM + 16, heads * half_rows), jnp.float32),
            pltpu.VMEM((2, half_rows // 128, query_width, 128), bf16),
            dma((15,)),
            dma((len(ARRIVALS),)),
            dma((2,)),
            dma((2 * experts,)),
            dma((2 * experts,)),
            dma((2, 4)),
            dma((experts,)),
            dma((8,)),
            dma((8,)),
            dma((5,)),
        ],
        compiler_params=pltpu.CompilerParams(
            collective_id=0, has_side_effects=True, vmem_limit_bytes=48 * 2**20
        ),
        cost_estimate=pl.CostEstimate(
            flops=20_000_000_000, bytes_accessed=20_000_000, transcendentals=27_000_000
        ),
        name="attention",
    )(queries, keyvals, send_grads, w_gate, w_up)


def expert_kernel(
    rows_ref,
    cot_ref,
    weights_ref,
    own_down_ref,
    hidden_ref,
    dispatch_ref,
    layer_ref,
    grad_gate_ref,
    grad_up_ref,
    grad_down_ref,
    rows_in,
    cot_in,
    weights_in,
    down_in,
    out_buf,
    out_in,
    parts,
    core_in,
    sums,
    half_up_in,
    half_down_in,
    full_up_in,
    full_down_in,
    push_send,
    push_recv,
    ring_send,
    ring_recv,
    weight_send,
    weight_recv,
    local_sem,
):
    zl, y, c, ex = (lax.axis_index(a) for a in (*SEQ, "exp"))
    experts = rows_ref.shape[0]
    capacity, width = rows_ref.shape[1:]
    tokens = 2 * experts * capacity
    core_peer = neighbour(c=1 - c)
    y_up = neighbour(y=lax.rem(y + 1, 4))
    y_down = neighbour(y=lax.rem(y + 3, 4))
    offsets = [(dz, de) for dz in range(2) for de in range(experts)]

    def peer(dz, de):
        return lax.rem(zl + dz, 2), lax.rem(ex + de, experts)

    def source(dz, de):
        return lax.rem(zl + 2 - dz, 2), lax.rem(ex + experts - de, experts)

    own_down = pltpu.make_async_copy(own_down_ref.at[0], down_in.at[c, y], local_sem.at[0])
    load_weights = pltpu.make_async_copy(weights_ref, weights_in, local_sem.at[3])
    load_cot = pltpu.make_async_copy(cot_ref, cot_in, local_sem.at[4])
    own_down.start()
    barrier = pltpu.get_barrier_semaphore()
    for dz, de in offsets[1:]:
        tz, te = peer(dz, de)
        pl.semaphore_signal(
            barrier, inc=1, device_id=neighbour(zl=tz, exp=te), device_id_type=MESH
        )
    for other in (core_peer, y_up, y_down):
        pl.semaphore_signal(barrier, inc=1, device_id=other, device_id_type=MESH)
    pl.semaphore_wait(barrier, len(offsets) + 2)

    def push(kind, index, src, dst, to):
        return pltpu.make_async_remote_copy(
            src_ref=src,
            dst_ref=dst,
            send_sem=push_send.at[kind, index],
            recv_sem=push_recv.at[kind, index],
            device_id=to,
            device_id_type=MESH,
        )

    def spread(kind, src_ref, dst_ref):
        own = pltpu.make_async_copy(src_ref.at[ex], dst_ref.at[zl, ex], local_sem.at[kind])
        own.start()
        sent = []
        for index, (dz, de) in enumerate(offsets):
            if index:
                tz, te = peer(dz, de)
                copy = push(
                    kind, index, src_ref.at[te], dst_ref.at[zl, ex], neighbour(zl=tz, exp=te)
                )
                copy.start()
                sent.append(copy)
        return own, sent

    def arrive(spread_copies):
        own, sent = spread_copies
        own.wait()
        for copy in sent:
            copy.wait_recv()

    rows_copies = spread(1, rows_ref, rows_in)

    def flat(ref):
        return ref[...].reshape(tokens, width)

    def ring(mat, stage, src, dst, to):
        return pltpu.make_async_remote_copy(
            src_ref=src,
            dst_ref=dst,
            send_sem=ring_send.at[mat, stage],
            recv_sem=ring_recv.at[mat, stage],
            device_id=to,
            device_id_type=MESH,
        )

    chunk = 512

    def partial(mat, first, second):
        turned = first.T
        for start in range(0, width, chunk):
            part = jnp.dot(
                turned, second[:, start : start + chunk], preferred_element_type=jnp.float32
            ).astype(jnp.bfloat16)
            parts[mat, :, :, :, pl.ds(start, chunk)] = part.reshape(2, 4, -1, chunk)

    started = []

    def go(copy):
        copy.start()
        started.append(copy)
        return copy

    def core_stage(mat):
        return go(ring(mat, 0, parts.at[mat, 1 - c], core_in.at[mat], core_peer))

    def wide(value):
        return value.astype(jnp.float32)

    half = parts.shape[3] // 2

    def half_stage(mat, core_copy):
        core_copy.wait_recv()
        sums[mat] = (wide(parts[mat, c]) + wide(core_in[mat])).astype(jnp.bfloat16)
        far = lax.rem(y + 2, 4)
        return (
            go(ring(mat, 1, sums.at[mat, far, pl.ds(0, half)], half_up_in.at[mat], y_up)),
            go(ring(mat, 2, sums.at[mat, far, pl.ds(half, half)], half_down_in.at[mat], y_down)),
        )

    def full_stage(mat, copies):
        above = lax.rem(y + 1, 4)
        below = lax.rem(y + 3, 4)
        copies[0].wait_recv()
        low = pl.ds(0, half)
        sums[mat, above, low] = (wide(sums[mat, above, low]) + wide(half_up_in[mat])).astype(
            jnp.bfloat16
        )
        first = go(ring(mat, 3, sums.at[mat, above], full_up_in.at[mat], y_up))
        copies[1].wait_recv()
        high = pl.ds(half, half)
        sums[mat, below, high] = (wide(sums[mat, below, high]) + wide(half_down_in[mat])).astype(
            jnp.bfloat16
        )
        return (first, go(ring(mat, 4, sums.at[mat, below], full_down_in.at[mat], y_down)))

    def finish(mat, copies, out_ref):
        for copy in copies:
            copy.wait_recv()
        out_ref[0] = (wide(sums[mat, y]) + wide(full_up_in[mat]) + wide(full_down_in[mat])).astype(
            jnp.bfloat16
        )

    def weight_copy(index, rows, dy, to):
        part = down_in.at[c, lax.rem(y + dy, 4), rows]
        return pltpu.make_async_remote_copy(
            src_ref=part,
            dst_ref=part,
            send_sem=weight_send.at[index],
            recv_sem=weight_recv.at[index],
            device_id=to,
            device_id_type=MESH,
        )

    own_down.wait()
    owned = down_in.shape[2]
    every, low, high = pl.ds(0, owned), pl.ds(0, owned // 2), pl.ds(owned // 2, owned // 2)
    weight_own = [
        go(weight_copy(0, every, 0, y_up)),
        go(weight_copy(1, every, 0, y_down)),
        go(weight_copy(2, every, 0, core_peer)),
    ]
    load_weights.start()
    load_cot.start()
    weight_own[0].wait_recv()
    weight_above = go(weight_copy(3, low, 3, y_up))
    weight_core = [go(weight_copy(5, every, 3, core_peer))]
    weight_own[1].wait_recv()
    weight_below = go(weight_copy(4, high, 1, y_down))
    weight_core.append(go(weight_copy(6, every, 1, core_peer)))
    weight_above.wait_recv()
    weight_below.wait_recv()
    weight_core.append(go(weight_copy(7, every, 2, core_peer)))
    for copy in (weight_own[2], *weight_core):
        copy.wait_recv()
    load_cot.wait()
    load_weights.wait()
    gate, up = (weights_in[n].reshape(-1, width) for n in range(2))
    down = down_in[...].reshape(-1, width)
    output_grads = flat(cot_in)
    hidden_grad = contract_cols(output_grads, down)
    arrive(rows_copies)
    expert_rows = flat(rows_in)
    gate_act = contract_cols(expert_rows, gate)
    up_act = contract_cols(expert_rows, up)
    hidden_units = swiglu_forward(gate_act, up_act)
    partial(0, hidden_units, output_grads)
    core_down = core_stage(0)
    gate_grad, up_grad = swiglu_backward(gate_act, up_act, hidden_grad)
    partial(1, gate_grad, expert_rows)
    core_gate = core_stage(1)
    half_down = half_stage(0, core_down)
    partial(2, up_grad, expert_rows)
    core_up = core_stage(2)
    half_gate = half_stage(1, core_gate)
    for start in range(0, width, chunk):
        out_buf[:, :, :, pl.ds(start, chunk)] = (
            jnp.dot(
                hidden_units,
                down[:, start : start + chunk],
                preferred_element_type=jnp.float32,
            )
            .astype(jnp.bfloat16)
            .reshape(2, experts, capacity, chunk)
        )
    own_out = pltpu.make_async_copy(out_buf.at[zl, ex], out_in.at[zl, ex], local_sem.at[2])
    own_out.start()
    back = []
    for index, (dz, de) in enumerate(offsets):
        if index:
            tz, te = peer(dz, de)
            copy = push(
                2, index, out_buf.at[tz, te], out_in.at[zl, ex], neighbour(zl=tz, exp=te)
            )
            copy.start()
            back.append(copy)
    full_down = full_stage(0, half_down)
    half_up = half_stage(2, core_up)
    full_gate = full_stage(1, half_gate)
    full_up = full_stage(2, half_up)
    finish(0, full_down, grad_down_ref)
    arrive((own_out, back))
    for start in range(0, width, chunk):
        cols = pl.ds(start, chunk)
        combined = sum(
            contract_rows(dispatch_ref[...], out_in[z, :, :, cols].reshape(-1, chunk))
            for z in range(2)
        )
        layer_ref[:, cols] = (wide(hidden_ref[:, cols]) + combined).astype(jnp.bfloat16)
    finish(1, full_gate, grad_gate_ref)
    finish(2, full_up, grad_up_ref)
    for copy in (*rows_copies[1], *back, *started):
        copy.wait_send()


def hand_on_kernel(*refs):
    for source, result in zip(refs[:4], refs[4:]):
        result[...] = source[...]


def expert_layer(send_rows, grad_rows, weights, w_down, hidden_state, dispatch_table):
    experts, capacity, width = send_rows.shape
    owned = weights.shape[3]
    token_count = hidden_state.shape[0]
    vmem = pl.BlockSpec(memory_space=pltpu.VMEM)
    anywhere = pl.BlockSpec(memory_space=pl.ANY)
    bf16 = jnp.bfloat16
    landing = pltpu.VMEM((2, experts, capacity, width), bf16)
    grad_shape = jax.ShapeDtypeStruct((1, owned, width), bf16)
    results = pl.pallas_call(
        expert_kernel,
        out_shape=(jax.ShapeDtypeStruct((token_count, width), bf16),) + (grad_shape,) * 3,
        in_specs=[anywhere] * 4 + [vmem] * 2,
        out_specs=(vmem,) * 4,
        scratch_shapes=[
            landing,
            landing,
            pltpu.VMEM(weights.shape, bf16),
            pltpu.VMEM((2, 4, owned, width), bf16),
            landing,
            landing,
            pltpu.VMEM((3, 2, 4, owned, width), bf16),
            pltpu.VMEM((3, 4, owned, width), bf16),
            pltpu.VMEM((3, 4, owned, width), bf16),
            pltpu.VMEM((3, owned // 2, width), bf16),
            pltpu.VMEM((3, owned // 2, width), bf16),
            pltpu.VMEM((3, owned, width), bf16),
            pltpu.VMEM((3, owned, width), bf16),
            pltpu.SemaphoreType.DMA((3, 2 * experts)),
            pltpu.SemaphoreType.DMA((3, 2 * experts)),
            pltpu.SemaphoreType.DMA((3, 5)),
            pltpu.SemaphoreType.DMA((3, 5)),
            pltpu.SemaphoreType.DMA((8,)),
            pltpu.SemaphoreType.DMA((8,)),
            pltpu.SemaphoreType.DMA((5,)),
        ],
        compiler_params=pltpu.CompilerParams(
            collective_id=1, has_side_effects=True, vmem_limit_bytes=56 * 2**20
        ),
        cost_estimate=pl.CostEstimate(
            flops=5_000_000_000, bytes_accessed=20_000_000, transcendentals=200_000
        ),
        name="experts",
    )(send_rows, grad_rows, weights, w_down, hidden_state, dispatch_table)
    return pl.pallas_call(
        hand_on_kernel,
        out_shape=[jax.ShapeDtypeStruct(r.shape, r.dtype) for r in results],
        in_specs=[vmem] * 4,
        out_specs=[vmem] * 4,
        name="hand_on",
    )(*results)


def local(
    resid,
    queries,
    keyvals,
    out_proj,
    norm_gain,
    token_ids,
    hash_table,
    w_gate,
    w_up,
    w_down,
    cotangent,
):
    token_count = resid.shape[0]
    model_width = resid.shape[1]
    expert_count = lax.axis_size("exp")
    capacity = token_count // expert_count
    expert_of = lax.gather(
        hash_table,
        token_ids[:, None],
        lax.GatherDimensionNumbers(
            offset_dims=(), collapsed_slice_dims=(0,), start_index_map=(0,)
        ),
        slice_sizes=(1,),
        mode=lax.GatherScatterMode.PROMISE_IN_BOUNDS,
    )
    order = jnp.arange(token_count, dtype=jnp.int32)
    same_earlier = (expert_of[:, None] == expert_of[None, :]) & (order[:, None] < order[None, :])
    slot_of = jnp.sum(same_earlier.astype(jnp.int32), axis=0)
    target = jnp.where(slot_of < capacity, expert_of * capacity + slot_of, -1)
    dispatch_table = (
        jnp.arange(expert_count * capacity, dtype=jnp.int32)[:, None] == target[None, :]
    ).astype(jnp.bfloat16)

    def placed(rows):
        return (
            jnp.dot(dispatch_table, rows, preferred_element_type=jnp.float32)
            .astype(jnp.bfloat16)
            .reshape(expert_count, capacity, model_width)
        )

    token_heads, grad_rows, weights = attend(
        queries.T, keyvals, placed(cotangent), w_gate, w_up
    )
    projected = contract_rows(token_heads.reshape(-1, token_count), out_proj)
    hidden_state = (resid.astype(jnp.float32) + projected).astype(jnp.bfloat16)
    widened = hidden_state.astype(jnp.float32)
    mean_square = jnp.mean(widened * widened, axis=1, keepdims=True)
    normed = (widened * lax.rsqrt(mean_square + norm_eps) * norm_gain.astype(jnp.float32)).astype(
        jnp.bfloat16
    )
    return expert_layer(
        placed(normed), grad_rows, weights, w_down, hidden_state, dispatch_table
    )


def solution(mesh):
    fine_mesh = Mesh(mesh.devices.reshape(2, 4, 2, 8), ("zl", "y", "c", "exp"))
    token_spec = P((*SEQ, "exp"), None)
    weight_spec = P("exp", SEQ, None)
    in_specs = (
        token_spec,
        P(SEQ, "exp"),
        P(SEQ, "exp"),
        P(),
        P(),
        P((*SEQ, "exp")),
        P(),
        weight_spec,
        weight_spec,
        weight_spec,
        token_spec,
    )
    out_specs = (token_spec, weight_spec, weight_spec, weight_spec)
    return jax.shard_map(
        local, mesh=fine_mesh, in_specs=in_specs, out_specs=out_specs, check_vma=False
    )
```
